512 devices in a mesh: lat: 16 (over z_lo, x), lon: 32 (over y, z_hi, core).
Axes of the slice: x: 4, y: 4, z: 16 (z_hi: 4, z_lo: 4; z = z_hi * 4 + z_lo), core: 2. Of those that a mesh axis runs over, the one named last changes fastest.
Arguments:
- tokens: bfloat16 [2, 384, 768, 512], P(None, 'lat', 'lon'), may hold values from -6 to 6
- attn_gain: float32 [512], replicated, may hold values from 0.1 to 1.9
- w_qkv: bfloat16 [512, 1536], P('lon'), may hold values from -1.5 to 1.5
- w_proj: bfloat16 [512, 512], P('lon'), may hold values from -0.25 to 0.25
- merge_gain: float32 [2048], replicated, may hold values from 0.1 to 1.9
- w_merge: bfloat16 [2048, 1024], P('lon'), may hold values from -0.125 to 0.125
Outputs:
- fine: bfloat16 [2, 384, 768, 512], P(None, 'lat', 'lon')
- coarse: bfloat16 [2, 192, 384, 1024], P(None, 'lat', 'lon')
The draws below stay inside these ranges and needn't reach their ends.
All inputs are finite; a program needn't handle non-finite values.
Results may differ from the reference program's by a relative error of at most 0.011.
Values may be sent and summed in bfloat16 or wider, within the bound.
No kernel may reach another device: no remote copies, remote signals or barrier semaphores. Data moves between devices by JAX's collectives and lax.ppermute only.
A program may use at most 64 MiB of HBM per device.

```python
import jax
import jax.numpy as jnp
from jax import lax

D = 512
HEADS = 8
LEV = 2
WL = 6
WW = 12
H = 384
W = 768


def draw_w_qkv(key, part):
    key = jax.random.fold_in(key, 7)
    subkeys = jax.random.split(key, 1)
    weights = jax.random.normal(subkeys[0], (D, 3 * D), jnp.float32) * D ** (-0.5)
    return jnp.clip(weights, -1.5, 1.5).astype(jnp.bfloat16)


def block_scale(rng, extent, cuts, smallest, largest):
    loudness = 1.0
    for dim, parts in cuts:
        draws = jax.random.uniform(jax.random.fold_in(jax.random.fold_in(rng, 6), dim), (parts,), jnp.float32, smallest / len(cuts), largest / len(cuts))
        loudness = loudness * jnp.repeat(jnp.exp(draws), extent[dim] // parts).reshape((-1,) + (1,) * (len(extent) - 1 - dim))
    return loudness


def noise(stream_key, dims, scale, bound, pieces=(), kind=jnp.bfloat16):
    loudness = block_scale(stream_key, dims, pieces, -0.22, 0.18) if pieces else 1.0
    values = jax.random.normal(stream_key, dims, jnp.float32) * scale * loudness
    return jnp.minimum(jnp.maximum(values, -bound), bound).astype(kind)


def setup_inputs(seed: int = 0) -> dict:
    streams_of = jax.random.split(jax.random.key(seed), 7)
    tokens = noise(streams_of[0], (LEV, H, W, D), 1.0, 6.0, ((1, 16), (2, 32)))
    attn_gain = jnp.clip(1.0 + 0.18 * jax.random.normal(streams_of[1], (D,), jnp.float32), 0.1, 1.9)
    w_qkv = draw_w_qkv(jax.random.fold_in(streams_of[6], 71), 0)
    w_proj = noise(streams_of[3], (D, D), D ** -0.5, 0.25, ((0, 32),))
    merge_gain = jnp.clip(1.0 + 0.18 * jax.random.normal(streams_of[4], (4 * D,), jnp.float32), 0.1, 1.9)
    w_merge = noise(streams_of[5], (4 * D, 2 * D), (4 * D) ** -0.5, 0.125, ((0, 32),))
    return dict(tokens=tokens, attn_gain=attn_gain, w_qkv=w_qkv, w_proj=w_proj, merge_gain=merge_gain, w_merge=w_merge)


eps = 1e-05

def layer_norm(values, gain):
    data = values.astype(jnp.float32)
    centred = data - lax.optimization_barrier(jnp.mean(data, axis=-1, keepdims=True))
    spread = lax.optimization_barrier(jnp.mean(centred * centred, axis=-1, keepdims=True))
    return centred * lax.rsqrt(spread + eps) * gain.astype(jnp.float32)

def window_attention(qkv, first_row, total_rows):
    levels, lat_rows, lon_cols, triple = qkv.shape
    width = triple // 3
    head = width // HEADS
    band_count = lat_rows // WL
    col_count = lon_cols // WW
    window = levels * WL * WW
    blocks = qkv.reshape(levels, band_count, WL, col_count, WW, 3, HEADS, head)
    blocks = blocks.transpose(5, 1, 3, 6, 0, 2, 4, 7).reshape(3, band_count, col_count, HEADS, window, head)
    query = blocks[0].astype(jnp.float32)
    keys = blocks[1].astype(jnp.float32)
    values = blocks[2].astype(jnp.float32)
    scores = jnp.einsum('abhqd,abhkd->abhqk', query, keys) * head ** (-0.5)
    rows = first_row + jnp.arange(lat_rows, dtype=jnp.int32)
    region = (rows >= total_rows - WL // 2).astype(jnp.int32).reshape(band_count, 1, WL, 1)
    region = jnp.broadcast_to(region, (band_count, levels, WL, WW)).reshape(band_count, window)
    same = region[:, :, None] == region[:, None, :]
    scores = jnp.where(same[:, None, None], scores, -1e+30)
    top = lax.optimization_barrier(jnp.max(scores, axis=-1, keepdims=True))
    expo = jnp.exp(scores - top)
    probs = (expo / lax.optimization_barrier(jnp.sum(expo, axis=-1, keepdims=True))).astype(jnp.bfloat16)
    attended = jnp.einsum('abhqk,abhkd->abhqd', probs.astype(jnp.float32), values).astype(jnp.bfloat16)
    attended = attended.reshape(band_count, col_count, HEADS, levels, WL, WW, head)
    return attended.transpose(3, 0, 4, 1, 5, 2, 6).reshape(levels, lat_rows, lon_cols, width)

def merge_rows(fine):
    levels, rows, cols, width = fine.shape
    grouped = fine.reshape(levels, rows // 2, 2, cols // 2, 2, width).transpose(0, 1, 3, 4, 2, 5)
    return grouped.reshape(levels, rows // 2, cols // 2, 4 * width)

def reference(tokens, attn_gain, w_qkv, w_proj, merge_gain, w_merge):
    levels, rows, cols, width = tokens.shape
    rolled = jnp.roll(tokens, (-(WL // 2), -(WW // 2)), axis=(1, 2))
    band_count = rows // WL
    blocks = rolled.reshape(levels, band_count, WL, cols, width).transpose(1, 0, 2, 3, 4)

    def one_band(item):
        index, block = item
        normed = layer_norm(block, attn_gain).astype(jnp.bfloat16)
        qkv = jnp.dot(normed.reshape(-1, width), w_qkv, preferred_element_type=jnp.float32)
        qkv = qkv.astype(jnp.bfloat16).reshape(levels, WL, cols, 3 * width)
        attended = window_attention(qkv, index * WL, rows)
        projected = jnp.dot(attended.reshape(-1, width), w_proj, preferred_element_type=jnp.float32)
        summed = block.astype(jnp.float32) + projected.reshape(block.shape)
        return summed.astype(jnp.bfloat16)
    outs = lax.map(one_band, (jnp.arange(band_count, dtype=jnp.int32), blocks))
    fine_rolled = outs.transpose(1, 0, 2, 3, 4).reshape(levels, rows, cols, width)
    fine = jnp.roll(fine_rolled, (WL // 2, WW // 2), axis=(1, 2))
    fine_blocks = fine.reshape(levels, band_count, WL, cols, width).transpose(1, 0, 2, 3, 4)

    def one_merge(block):
        merged = layer_norm(merge_rows(block), merge_gain).astype(jnp.bfloat16)
        result = jnp.dot(merged.reshape(-1, 4 * width), w_merge, preferred_element_type=jnp.float32)
        return result.astype(jnp.bfloat16).reshape(levels, WL // 2, cols // 2, 2 * width)
    coarse = lax.map(one_merge, fine_blocks)
    coarse = coarse.transpose(1, 0, 2, 3, 4).reshape(levels, rows // 2, cols // 2, 2 * width)
    return (fine, coarse)
```

```python
import functools
import numpy as np
import jax
import jax.numpy as jnp
from jax import lax
from jax.sharding import Mesh, PartitionSpec as P
from jax.experimental import pallas as pl
from jax.experimental.pallas import tpu as pltpu

HEADS = 8
WL = 6
WW = 12
eps = 1e-05
f32 = jnp.float32
bf16 = jnp.bfloat16


def centre_order():
    order = []
    for first, last in ((0, 6), (6, 18), (18, 24)):
        for l in range(2):
            for r in range(6):
                order += [(l * 6 + r) * 24 + c for c in range(first, last)]
    return np.array(order)


def one_hot(order, n):
    return (order[:, None] == np.arange(n)[None, :]).astype(jnp.bfloat16)


def row_half():
    side = [r // 3 for l in range(2) for r in range(6) for c in range(6)]
    mid = [r // 3 for l in range(2) for r in range(6) for c in range(12)]
    return np.array(side + side + mid + side + side, np.float32)


def merge_order():
    return np.array([i * 24 + 2 * j + p for p in range(2) for i in range(12) for j in range(12)])


def dot(a, b, ca=1, cb=0):
    return lax.dot_general(a, b, (((ca,), (cb,)), ((), ())), preferred_element_type=f32)


def norm(x, gain):
    centred = x - jnp.mean(x, axis=-1, keepdims=True)
    spread = jnp.mean(centred * centred, axis=-1, keepdims=True)
    return centred * lax.rsqrt(spread + eps) * gain


def attend(q, k, v, bias, low):
    n = q.shape[0]
    out = []
    ones = jnp.ones((k.shape[0], 128), bf16)
    zero = jnp.zeros((), bf16)
    for pair in range(HEADS // 2):
        cols = slice(pair * 128, pair * 128 + 128)
        qp = q[:, cols]
        both = jnp.concatenate([jnp.where(low, qp, zero), jnp.where(low, zero, qp)], axis=0)
        s = dot(both, k[:, cols], 1, 1)
        s = s + jnp.concatenate([bias, bias], axis=0)
        e = jnp.exp(s - jnp.max(s, axis=-1, keepdims=True)).astype(bf16)
        o = dot(e, jnp.concatenate([v[:, cols], ones], axis=1))
        o = o[:, :128] / o[:, 128:]
        out.append(jnp.where(low, o[:n], o[n:]))
    return jnp.concatenate(out, axis=1)


def block_kernel(place_ref, mid_ref, left_ref, right_ref, gain_ref, own_ref, sibling_ref, perm_ref, back_ref, mask_ref,
                 fine_ref, weights, sems):
    band = pl.program_id(0)
    bands = pl.num_programs(0)

    @pl.when(band == 0)
    def _():
        core = place_ref[2]
        copies = [pltpu.make_async_copy(ref, weights.at[:, at], sems.at[n])
                  for n, (ref, at) in enumerate(((own_ref, core), (sibling_ref, 1 - core)))]
        for copy in copies:
            copy.start()
        for copy in copies:
            copy.wait()

    gain = gain_ref[...]
    raw = mid_ref[:, pl.ds(band * WL, WL)].reshape(288, 512)
    centre = norm(raw.astype(f32), gain).astype(bf16)
    centre = dot(perm_ref[...], centre)
    left = norm(left_ref[...].reshape(72, 512).astype(f32), gain)
    right = norm(right_ref[...].reshape(72, 512).astype(f32), gain)
    tokens = jnp.concatenate([left, centre, right], axis=0).astype(bf16)
    columns = [weights[:, :, :, n * 512:n * 512 + 512].reshape(512, 512) for n in range(4)]
    q = dot(centre.astype(bf16), columns[0]).astype(bf16) * jnp.asarray(0.125, bf16)
    k = dot(tokens, columns[1]).astype(bf16)
    v = dot(tokens, columns[2]).astype(bf16)
    low = lax.broadcasted_iota(jnp.int32, (1, 128), 1) < 64
    edge = ((place_ref[0] == 0) & (band == 0)) | ((place_ref[0] == place_ref[1]) & (band == bands - 1))
    scale = jnp.where(edge, 1.0, 0.0).astype(f32)
    mask = mask_ref[...] * scale
    spans = ((0, 72, 0), (72, 216, 144), (216, 288, 288))
    att = [attend(q[a:b], k[c:c + 144], v[c:c + 144], mask[a:b], low) for a, b, c in spans]
    att = jnp.concatenate(att, axis=0).astype(bf16)
    att = dot(back_ref[...], att).astype(bf16)
    out = dot(att, columns[3]) + raw.astype(f32)
    out = out.astype(bf16).reshape(2, WL, 24, 512)

    @pl.when(band > 0)
    def _():
        fine_ref[:, pl.ds(band * WL - 3, 3)] = out[:, :3]

    @pl.when(band < bands - 1)
    def _():
        fine_ref[:, pl.ds(band * WL, 3)] = out[:, 3:]


def norm_kernel(fine_ref, gain_ref, sel_ref, merged_ref):
    for l in range(2):
        parts = {}
        for p in range(2):
            rows = jnp.concatenate([fine_ref[l, 2 * i + p] for i in range(12)], axis=0)
            both = dot(sel_ref[...], rows)
            parts[p, 0] = both[:144]
            parts[p, 1] = both[144:]
        order = [parts[0, 0], parts[1, 0], parts[0, 1], parts[1, 1]]
        mean = sum(jnp.sum(a, axis=-1, keepdims=True) for a in order) * (1 / 2048)
        centred = [a - mean for a in order]
        spread = sum(jnp.sum(a * a, axis=-1, keepdims=True) for a in centred) * (1 / 2048)
        scale = lax.rsqrt(spread + eps)
        for n, a in enumerate(centred):
            cols = slice(n * 512, n * 512 + 512)
            merged_ref[l * 144:l * 144 + 144, cols] = (a * scale * gain_ref[:, cols]).astype(bf16)


def merge_kernel(merged_ref, w_ref, coarse_ref):
    coarse_ref[...] = dot(merged_ref[...], w_ref[...]).astype(bf16)


def whole(shape):
    return pl.BlockSpec(shape, lambda *_: (0,) * len(shape))


def attention_block(mid, left, right, gain, own, sibling, place):
    order = centre_order()
    perm = one_hot(order, 288)
    half = row_half()
    key_half = [half[0:144], half[144:288], half[288:432]]
    query_half = half[72:360]
    spans = ((0, 72), (72, 216), (216, 288))
    mask = np.concatenate([
        np.where(query_half[a:b, None] == key_half[n][None, :], 0.0, -1e30).astype(np.float32)
        for n, (a, b) in enumerate(spans)])
    bands = mid.shape[1] // WL
    return pl.pallas_call(
        block_kernel,
        grid=(bands,),
        in_specs=[
            pl.BlockSpec(memory_space=pltpu.SMEM),
            whole(mid.shape),
            pl.BlockSpec((1, 72, 512), lambda b: (b, 0, 0)),
            pl.BlockSpec((1, 72, 512), lambda b: (b, 0, 0)),
            whole((1, 512)),
            pl.BlockSpec(memory_space=pl.ANY),
            pl.BlockSpec(memory_space=pl.ANY),
            whole((288, 288)),
            whole((288, 288)),
            whole((288, 144)),
        ],
        out_specs=whole((2, 24, 24, 512)),
        out_shape=jax.ShapeDtypeStruct((2, 24, 24, 512), bf16),
        scratch_shapes=[pltpu.VMEM((own.shape[0], 2) + own.shape[1:], bf16), pltpu.SemaphoreType.DMA((2,))],
        compiler_params=pltpu.CompilerParams(vmem_limit_bytes=48 << 20),
        cost_estimate=pl.CostEstimate(flops=5_200_000_000, bytes_accessed=8 << 20, transcendentals=2_500_000),
        name="attention_block",
    )(place, mid, left, right, gain.reshape(1, 512), own, sibling, jnp.asarray(perm), jnp.asarray(perm.T), jnp.asarray(mask))


def merge_norm(fine, gain):
    sel = one_hot(merge_order(), 288)
    return pl.pallas_call(
        norm_kernel,
        out_shape=jax.ShapeDtypeStruct((288, 2048), bf16),
        compiler_params=pltpu.CompilerParams(vmem_limit_bytes=32 << 20),
        cost_estimate=pl.CostEstimate(flops=340_000_000, bytes_accessed=3 << 20, transcendentals=300),
        name="merge_norm",
    )(fine, gain.reshape(1, 2048), jnp.asarray(sel))


def merge_product(merged, w):
    return pl.pallas_call(
        merge_kernel,
        grid=(4,),
        in_specs=[whole((288, 2048)), pl.BlockSpec((2048, 256), lambda n: (0, n))],
        out_specs=pl.BlockSpec((288, 256), lambda n: (0, n)),
        out_shape=jax.ShapeDtypeStruct((288, 1024), bf16),
        compiler_params=pltpu.CompilerParams(vmem_limit_bytes=32 << 20),
        cost_estimate=pl.CostEstimate(flops=1_200_000_000, bytes_accessed=6 << 20, transcendentals=0),
        name="merge_product",
    )(merged, w)


LAT = ("zl", "x")
LON = ("y", "zh", "c")


def shift(block, axes, distance):
    devices = range(lax.axis_size(axes))
    route = [((i - distance) % len(devices), i) for i in devices]
    return lax.ppermute(block, axes, route)


def band_rows(piece):
    bands = piece.shape[1] // WL
    return piece.reshape(2, bands, WL, 6, 512).transpose(1, 0, 2, 3, 4).reshape(bands, 72, 512)


def on_device(tokens, attn_gain, w_qkv, w_proj, merge_gain, w_merge):
    above = shift(tokens[:, -3:], LAT, 1)
    below = shift(tokens[:, :3], LAT, -1)
    mid = jnp.concatenate([above, tokens, below], axis=1)
    left = shift(band_rows(mid[:, :, -6:]), LON, 1)
    right = shift(band_rows(mid[:, :, :6]), LON, -1)
    rows = w_qkv.shape[0]
    packed = jnp.concatenate([w_qkv, w_proj], axis=1)
    packed = lax.all_gather(packed, "zh")
    qkv_part = lax.all_gather(packed[:, :, :1536], "y")
    proj_part = lax.all_gather(packed[:, :, 1536:], "y")
    own = jnp.concatenate([qkv_part, proj_part], axis=-1).reshape(-1, rows, 2048)
    sibling = shift(own, "c", 1)
    place = jnp.stack([lax.axis_index(LAT), lax.axis_size(LAT) - 1, lax.axis_index("c")]).astype(jnp.int32)
    fine = attention_block(mid, left, right, attn_gain, own, sibling, place)
    merged = merge_norm(fine, merge_gain)
    coarse = merge_product(merged, lax.all_gather(w_merge, LON, axis=0, tiled=True))
    return fine, coarse.reshape(2, 12, 12, 1024)


def solution(mesh):
    lat, lon = mesh.shape["lat"], mesh.shape["lon"]
    fine_mesh = Mesh(mesh.devices.reshape(lat // 4, 4, 4, lon // 8, 2), LAT + LON)
    in_specs = (P(None, LAT, LON, None), P(), P(LON, None), P(LON, None), P(), P(LON, None))
    out_specs = (P(None, LAT, LON, None), P(None, LAT, LON, None))
    return jax.shard_map(
        on_device, mesh=fine_mesh, in_specs=in_specs, out_specs=out_specs, check_vma=False
    )
```

```python
import functools
import numpy as np
import jax
import jax.numpy as jnp
from jax import lax
from jax.sharding import Mesh, PartitionSpec as P
from jax.experimental import pallas as pl
from jax.experimental.pallas import tpu as pltpu

HEADS = 8
WL = 6
WW = 12
eps = 1e-05
f32 = jnp.float32
bf16 = jnp.bfloat16


def centre_order():
    order = []
    for first, last in ((0, 6), (6, 18), (18, 24)):
        for l in range(2):
            for r in range(6):
                order += [(l * 6 + r) * 24 + c for c in range(first, last)]
    return np.array(order)


def one_hot(order, n):
    return (order[:, None] == np.arange(n)[None, :]).astype(jnp.bfloat16)


def row_half():
    side = [r // 3 for l in range(2) for r in range(6) for c in range(6)]
    mid = [r // 3 for l in range(2) for r in range(6) for c in range(12)]
    return np.array(side + side + mid + side + side, np.float32)


def merge_order():
    return np.array([i * 24 + 2 * j + p for p in range(2) for i in range(12) for j in range(12)])


def dot(a, b, ca=1, cb=0):
    return lax.dot_general(a, b, (((ca,), (cb,)), ((), ())), preferred_element_type=f32)


def norm(x, gain):
    centred = x - jnp.mean(x, axis=-1, keepdims=True)
    spread = jnp.mean(centred * centred, axis=-1, keepdims=True)
    return centred * lax.rsqrt(spread + eps) * gain


def attend(q, k, v, bias, low):
    n = q.shape[0]
    out = []
    ones = jnp.ones((k.shape[0], 128), bf16)
    zero = jnp.zeros((), bf16)
    for pair in range(HEADS // 2):
        cols = slice(pair * 128, pair * 128 + 128)
        qp = q[:, cols]
        both = jnp.concatenate([jnp.where(low, qp, zero), jnp.where(low, zero, qp)], axis=0)
        s = dot(both, k[:, cols], 1, 1)
        s = s + jnp.concatenate([bias, bias], axis=0)
        e = jnp.exp(s - jnp.max(s, axis=-1, keepdims=True)).astype(bf16)
        o = dot(e, jnp.concatenate([v[:, cols], ones], axis=1))
        o = o[:, :128] / o[:, 128:]
        out.append(jnp.where(low, o[:n], o[n:]))
    return jnp.concatenate(out, axis=1)


def pack_kernel(place_ref, qkv_ref, proj_ref, merge_ref, out_ref):
    for n in range(3):
        out_ref[n] = qkv_ref[:, n * 512:n * 512 + 512]
    out_ref[3] = proj_ref[...]
    quarter = merge_ref[pl.ds(pl.multiple_of(place_ref[3] * 16, 16), 16), :]
    out_ref[4] = quarter[:, :512]
    out_ref[5] = quarter[:, 512:]


def edge_kernel(place_ref, tokens_ref, above_ref, below_ref, sel_ref, outer_ref, inner_ref):
    first = place_ref[2] == 0
    for band in range(5):
        parts = []
        if band > 0:
            parts.append(tokens_ref[:, band * WL - 3:band * WL])
        else:
            parts.append(above_ref[...])
        if band < 4:
            parts.append(tokens_ref[:, band * WL:band * WL + 3])
        else:
            parts.append(below_ref[...])
        rows = jnp.concatenate(parts, axis=1).reshape(288, 512)
        both = dot(sel_ref[...], rows)
        left, right = both[:72], both[72:]
        outer_ref[band] = jnp.where(first, left, right).astype(bf16)
        inner_ref[band] = jnp.where(first, right, left).astype(bf16)


def block_kernel(place_ref, tokens_ref, above_ref, below_ref, outer_ref, inner_ref, gain_ref, own_qkv_ref, own_rest_ref, sibling_qkv_ref,
                 sibling_rest_ref, perm_ref, back_ref, mask_ref, fine_ref, mid_ref, weights, sems):
    band = pl.program_id(0)
    bands = pl.num_programs(0)
    core = place_ref[2]

    @pl.when(band == 0)
    def _():
        copies = [
            pltpu.make_async_copy(above_ref, mid_ref.at[:, 0:3], sems.at[8]),
            pltpu.make_async_copy(tokens_ref, mid_ref.at[:, 3:27], sems.at[9]),
            pltpu.make_async_copy(below_ref, mid_ref.at[:, 27:30], sems.at[10]),
        ]
        for m, (qkv, rest, at) in enumerate(((own_qkv_ref, own_rest_ref, core), (sibling_qkv_ref, sibling_rest_ref, 1 - core))):
            for n in range(4):
                source = qkv.at[:, n] if n < 3 else rest.at[:, 0]
                copies.append(pltpu.make_async_copy(source, weights.at[n, :, at], sems.at[4 * m + n]))
        for copy in copies:
            copy.start()
        for copy in copies:
            copy.wait()

    gain = gain_ref[...]
    raw = mid_ref[:, pl.ds(band * WL, WL)].reshape(288, 512)
    centre = norm(raw.astype(f32), gain).astype(bf16)
    centre = dot(perm_ref[...], centre)
    outer = norm(outer_ref[...].reshape(72, 512).astype(f32), gain)
    inner = norm(inner_ref[...].reshape(72, 512).astype(f32), gain)
    left = jnp.where(core == 0, outer, inner)
    right = jnp.where(core == 0, inner, outer)
    tokens = jnp.concatenate([left, centre, right], axis=0).astype(bf16)
    columns = [weights[n].reshape(512, 512) for n in range(4)]
    q = dot(centre.astype(bf16), columns[0]).astype(bf16) * jnp.asarray(0.125, bf16)
    k = dot(tokens, columns[1]).astype(bf16)
    v = dot(tokens, columns[2]).astype(bf16)
    low = lax.broadcasted_iota(jnp.int32, (1, 128), 1) < 64
    edge = ((place_ref[0] == 0) & (band == 0)) | ((place_ref[0] == place_ref[1]) & (band == bands - 1))
    scale = jnp.where(edge, 1.0, 0.0).astype(f32)
    mask = mask_ref[...] * scale
    spans = ((0, 72, 0), (72, 216, 144), (216, 288, 288))
    att = [attend(q[a:b], k[c:c + 144], v[c:c + 144], mask[a:b], low) for a, b, c in spans]
    att = jnp.concatenate(att, axis=0).astype(bf16)
    att = dot(back_ref[...], att).astype(bf16)
    out = dot(att, columns[3]) + raw.astype(f32)
    out = out.astype(bf16).reshape(2, WL, 24, 512)

    @pl.when(band > 0)
    def _():
        fine_ref[:, pl.ds(band * WL - 3, 3)] = out[:, :3]

    @pl.when(band < bands - 1)
    def _():
        fine_ref[:, pl.ds(band * WL, 3)] = out[:, 3:]


def merge_kernel(place_ref, fine_ref, gain_ref, sel_ref, own_ref, sibling_ref, own_far_ref, sibling_far_ref, coarse_ref,
                 weights, merged, sems):
    core = place_ref[2]
    x = place_ref[3]
    copies = []
    for col in range(2):
        for at, near, far in ((core, own_ref, own_far_ref), (1 - core, sibling_ref, sibling_far_ref)):
            side = 0 if near is own_ref else 1
            copies.append(pltpu.make_async_copy(near.at[:, 1 + col], weights.at[col, :, at, x], sems.at[col, side, 0]))
            for n, step in enumerate((3, 1, 2)):
                there = lax.rem(x + step, 4)
                copies.append(pltpu.make_async_copy(far.at[n, :, col], weights.at[col, :, at, there], sems.at[col, side, n + 1]))
    for copy in copies:
        copy.start()
    for l in range(2):
        parts = {}
        for p in range(2):
            rows = jnp.concatenate([fine_ref[l, 2 * i + p] for i in range(12)], axis=0)
            both = dot(sel_ref[...], rows)
            parts[p, 0] = both[:144]
            parts[p, 1] = both[144:]
        order = [parts[0, 0], parts[1, 0], parts[0, 1], parts[1, 1]]
        mean = sum(jnp.sum(a, axis=-1, keepdims=True) for a in order) * (1 / 2048)
        centred = [a - mean for a in order]
        spread = sum(jnp.sum(a * a, axis=-1, keepdims=True) for a in centred) * (1 / 2048)
        scale = lax.rsqrt(spread + eps)
        for n, a in enumerate(centred):
            cols = slice(n * 512, n * 512 + 512)
            merged[l * 144:l * 144 + 144, cols] = (a * scale * gain_ref[:, cols]).astype(bf16)
    for copy in copies:
        copy.wait()
    for col in range(2):
        part = dot(merged[...], weights[col].reshape(2048, 512))
        coarse_ref[:, col * 512:col * 512 + 512] = part.astype(bf16)


def whole(shape):
    return pl.BlockSpec(shape, lambda *_: (0,) * len(shape))


def attention_block(tokens, above, below, outer, inner, gain, own_qkv, own_rest, sibling_qkv, sibling_rest, place):
    order = centre_order()
    perm = one_hot(order, 288)
    half = row_half()
    key_half = [half[0:144], half[144:288], half[288:432]]
    query_half = half[72:360]
    spans = ((0, 72), (72, 216), (216, 288))
    mask = np.concatenate([
        np.where(query_half[a:b, None] == key_half[n][None, :], 0.0, -1e30).astype(np.float32)
        for n, (a, b) in enumerate(spans)])
    bands = 5
    anywhere = pl.BlockSpec(memory_space=pl.ANY)
    return pl.pallas_call(
        block_kernel,
        grid=(bands,),
        in_specs=[
            pl.BlockSpec(memory_space=pltpu.SMEM),
            anywhere,
            anywhere,
            anywhere,
            pl.BlockSpec((1, 72, 512), lambda b: (b, 0, 0)),
            pl.BlockSpec((1, 72, 512), lambda b: (b, 0, 0)),
            whole((1, 512)),
            anywhere,
            anywhere,
            anywhere,
            anywhere,
            whole((288, 288)),
            whole((288, 288)),
            whole((288, 144)),
        ],
        out_specs=whole((2, 24, 24, 512)),
        out_shape=jax.ShapeDtypeStruct((2, 24, 24, 512), bf16),
        scratch_shapes=[
            pltpu.VMEM((2, 30, 24, 512), bf16),
            pltpu.VMEM((4, 16, 2, 16, 512), bf16),
            pltpu.SemaphoreType.DMA((11,)),
        ],
        compiler_params=pltpu.CompilerParams(vmem_limit_bytes=48 << 20),
        cost_estimate=pl.CostEstimate(flops=5_200_000_000, bytes_accessed=8 << 20, transcendentals=2_500_000),
        name="attention_block",
    )(place, tokens, above, below, outer, inner, gain.reshape(1, 512), own_qkv, own_rest, sibling_qkv, sibling_rest, jnp.asarray(perm), jnp.asarray(perm.T), jnp.asarray(mask))


def pack(w_qkv, w_proj, w_merge, place):
    vmem = pl.BlockSpec(memory_space=pltpu.VMEM)
    return pl.pallas_call(
        pack_kernel,
        in_specs=[pl.BlockSpec(memory_space=pltpu.SMEM), vmem, vmem, vmem],
        out_specs=vmem,
        out_shape=jax.ShapeDtypeStruct((6, 16, 512), bf16),
        name="pack_weights",
    )(place, w_qkv, w_proj, w_merge)


def edges(tokens, above, below, place):
    cols = list(range(6)), list(range(18, 24))
    order = np.array([(l * 6 + r) * 24 + c for side in cols for l in range(2) for r in range(6) for c in side])
    vmem = pl.BlockSpec(memory_space=pltpu.VMEM)
    shape = jax.ShapeDtypeStruct((5, 72, 512), bf16)
    return pl.pallas_call(
        edge_kernel,
        in_specs=[pl.BlockSpec(memory_space=pltpu.SMEM), vmem, vmem, vmem, vmem],
        out_specs=(vmem, vmem),
        out_shape=(shape, shape),
        compiler_params=pltpu.CompilerParams(vmem_limit_bytes=32 << 20),
        cost_estimate=pl.CostEstimate(flops=212_000_000, bytes_accessed=3 << 20, transcendentals=0),
        name="edge_rows",
    )(place, tokens, above, below, jnp.asarray(one_hot(order, 288)))


def merge_block(fine, gain, own, sibling, own_far, sibling_far, place):
    sel = one_hot(merge_order(), 288)
    vmem = pl.BlockSpec(memory_space=pltpu.VMEM)
    anywhere = pl.BlockSpec(memory_space=pl.ANY)
    return pl.pallas_call(
        merge_kernel,
        in_specs=[pl.BlockSpec(memory_space=pltpu.SMEM), vmem, vmem, vmem] + [anywhere] * 4,
        out_shape=jax.ShapeDtypeStruct((288, 1024), bf16),
        scratch_shapes=[
            pltpu.VMEM((2, own.shape[0], 2, 4) + own.shape[2:], bf16),
            pltpu.VMEM((288, 2048), bf16),
            pltpu.SemaphoreType.DMA((2, 2, 4)),
        ],
        compiler_params=pltpu.CompilerParams(vmem_limit_bytes=40 << 20),
        cost_estimate=pl.CostEstimate(flops=1_540_000_000, bytes_accessed=8 << 20, transcendentals=300),
        name="merge_block",
    )(place, fine, gain.reshape(1, 2048), jnp.asarray(sel), own, sibling, own_far, sibling_far)


LAT = ("zl", "x")
LON = ("y", "zh", "c")


def shift(block, axes, distance):
    devices = range(lax.axis_size(axes))
    route = [((i - distance) % len(devices), i) for i in devices]
    return lax.ppermute(block, axes, route)


def between_chips(block):
    devices = range(lax.axis_size(LON))
    return lax.ppermute(block, LON, [(i, (i + (1 if i % 2 else -1)) % len(devices)) for i in devices])


def on_device(tokens, attn_gain, w_qkv, w_proj, merge_gain, w_merge):
    place = jnp.stack([lax.axis_index(LAT), lax.axis_size(LAT) - 1, lax.axis_index("c"), lax.axis_index("x")]).astype(jnp.int32)
    above = shift(tokens[:, -3:], LAT, 1)
    below = shift(tokens[:, :3], LAT, -1)
    packed = lax.all_gather(pack(w_qkv, w_proj, w_merge, place), "zh")
    packed, above, below = lax.optimization_barrier((packed, above, below))
    outer, inner = edges(tokens, above, below, place)
    outer = between_chips(outer)
    inner = shift(inner, "c", 1)
    rest = lax.all_gather(packed[:, 3:], "y").reshape(16, 3, 16, 512)
    rest, outer, inner = lax.optimization_barrier((rest, outer, inner))
    sibling_rest = shift(rest, "c", 1)
    merge_own = rest[:, 1:]
    before = shift(merge_own, "x", 1)
    after = shift(merge_own, "x", -1)
    qkv = lax.all_gather(packed[:, :3], "y").reshape(16, 3, 16, 512)
    before, after, sibling_rest, qkv = lax.optimization_barrier((before, after, sibling_rest, qkv))
    sibling_qkv = shift(qkv, "c", 1)
    across = [shift(before[:8], "x", 1), shift(after[8:], "x", -1)]
    own_far = jnp.stack([before, after, jnp.concatenate(across, axis=0)])
    sibling_far = shift(own_far, "c", 1)
    fine = attention_block(tokens, above, below, outer, inner, attn_gain, qkv, rest, sibling_qkv, sibling_rest, place)
    coarse = merge_block(fine, merge_gain, rest, sibling_rest, own_far, sibling_far, place)
    return fine, coarse.reshape(2, 12, 12, 1024)


def solution(mesh):
    lat, lon = mesh.shape["lat"], mesh.shape["lon"]
    fine_mesh = Mesh(mesh.devices.reshape(lat // 4, 4, 4, lon // 8, 2), LAT + LON)
    in_specs = (P(None, LAT, LON, None), P(), P(LON, None), P(LON, None), P(), P(LON, None))
    out_specs = (P(None, LAT, LON, None), P(None, LAT, LON, None))
    return jax.shard_map(
        on_device, mesh=fine_mesh, in_specs=in_specs, out_specs=out_specs, check_vma=False
    )
```

```python
import numpy as np
import jax
import jax.numpy as jnp
from jax import lax
from jax.sharding import Mesh, PartitionSpec as P
from jax.experimental import pallas as pl
from jax.experimental.pallas import tpu as pltpu

HEADS = 8
WL = 6
eps = 1e-05
f32 = jnp.float32
bf16 = jnp.bfloat16
LAT = ("zl", "x")
LON = ("y", "zh", "c")
VMEM = pl.BlockSpec(memory_space=pltpu.VMEM)
ANY = pl.BlockSpec(memory_space=pl.ANY)


def centre_order():
    order = []
    for first, last in ((0, 6), (6, 18), (18, 24)):
        for l in range(2):
            for r in range(6):
                order += [(l * 6 + r) * 24 + c for c in range(first, last)]
    return np.array(order)


def one_hot(order, n):
    return (order[:, None] == np.arange(n)[None, :]).astype(jnp.bfloat16)


def row_half():
    side = [r // 3 for l in range(2) for r in range(6) for c in range(6)]
    mid = [r // 3 for l in range(2) for r in range(6) for c in range(12)]
    return np.array(side + side + mid + side + side, np.float32)


def edge_mask():
    half = row_half()
    spans = ((0, 72), (72, 216), (216, 288))
    return np.concatenate([
        np.where(half[72 + a:72 + b, None] == half[None, n * 144:n * 144 + 144], 0.0, -1e30).astype(np.float32)
        for n, (a, b) in enumerate(spans)])


def merge_order():
    return np.array([i * 24 + 2 * j + p for p in range(2) for i in range(12) for j in range(12)])


def dot(a, b, ca=1, cb=0):
    return lax.dot_general(a, b, (((ca,), (cb,)), ((), ())), preferred_element_type=f32)


def norm(x, gain):
    centred = x - jnp.mean(x, axis=-1, keepdims=True)
    spread = jnp.mean(centred * centred, axis=-1, keepdims=True)
    return centred * lax.rsqrt(spread + eps) * gain


def x_slots(x):
    pair = x + 1 - 2 * lax.rem(x, 2)
    return ((x, pair), (3 - x, 3 - pair))


def pack_kernel(qkv_ref, proj_ref, merge_ref, out_ref):
    for n in range(3):
        out_ref[n] = qkv_ref[:, n * 512:n * 512 + 512]
    out_ref[3] = proj_ref[...]
    quarter = merge_ref[pl.ds(pl.multiple_of(lax.axis_index("x") * 16, 16), 16), :]
    out_ref[4] = quarter[:, :512]
    out_ref[5] = quarter[:, 512:]


def edge_kernel(tokens_ref, above_ref, below_ref, outer_ref, inner_ref):
    first = lax.axis_index("c") == 0
    o = lax.broadcasted_iota(jnp.int32, (144, 288), 0)
    side = (o * 911) >> 16
    lr = ((o - side * 72) * 10923) >> 16
    col = o - side * 72 - lr * 6 + side * 18
    sel = jnp.where(lax.broadcasted_iota(jnp.int32, (144, 288), 1) == lr * 24 + col, 1.0, 0.0).astype(bf16)
    for band in range(5):
        upper = tokens_ref[:, band * WL - 3:band * WL] if band > 0 else above_ref[...]
        lower = tokens_ref[:, band * WL:band * WL + 3] if band < 4 else below_ref[...]
        rows = jnp.concatenate([upper, lower], axis=1).reshape(288, 512)
        both = dot(sel, rows)
        left, right = both[:72], both[72:]
        outer_ref[band] = jnp.where(first, left, right).astype(bf16)
        inner = jnp.concatenate([jnp.where(first, right, left), jnp.zeros((8, 512), f32)], axis=0)
        inner_ref[band * 5:band * 5 + 5] = inner.astype(bf16).reshape(5, 16, 512)
    inner_ref[25:] = jnp.zeros((7, 16, 512), bf16)


def attend(q, k, v, bias, low):
    n = q.shape[0]
    out = []
    ones = jnp.ones((k.shape[0], 128), bf16)
    zero = jnp.zeros((), bf16)
    for pair in range(HEADS // 2):
        cols = slice(pair * 128, pair * 128 + 128)
        qp = q[:, cols]
        both = jnp.concatenate([jnp.where(low, qp, zero), jnp.where(low, zero, qp)], axis=0)
        s = dot(both, k[:, cols], 1, 1)
        s = s + jnp.concatenate([bias, bias], axis=0)
        e = jnp.exp(s - jnp.max(s, axis=-1, keepdims=True)).astype(bf16)
        o = dot(e, jnp.concatenate([v[:, cols], ones], axis=1))
        o = o[:, :128] / o[:, 128:]
        out.append(jnp.where(low, o[:n], o[n:]))
    return jnp.concatenate(out, axis=1)


def merge_norm(fine_ref, gain_ref, sel_ref, merged_ref):
    for l in range(2):
        parts = {}
        for p in range(2):
            rows = jnp.concatenate([fine_ref[l, 2 * i + p] for i in range(12)], axis=0)
            both = dot(sel_ref[...], rows)
            parts[p, 0] = both[:144]
            parts[p, 1] = both[144:]
        order = [parts[0, 0], parts[1, 0], parts[0, 1], parts[1, 1]]
        mean = sum(jnp.sum(a, axis=-1, keepdims=True) for a in order) * (1 / 2048)
        centred = [a - mean for a in order]
        spread = sum(jnp.sum(a * a, axis=-1, keepdims=True) for a in centred) * (1 / 2048)
        scale = lax.rsqrt(spread + eps)
        for n, a in enumerate(centred):
            cols = slice(n * 512, n * 512 + 512)
            merged_ref[l * 144:l * 144 + 144, cols] = (a * scale * gain_ref[:, cols]).astype(bf16)


def block_kernel(tokens_ref, above_ref, below_ref, outer_ref, gain_ref, own_qkv_ref, own_rest_ref, sibling_ref,
                 perm_ref, back_ref, mask_ref, merge_gain_ref, sel_ref, fine_ref, merged_ref, mid_ref, inner_ref, weights, sems):
    band = pl.program_id(0)
    bands = pl.num_programs(0)
    core = lax.axis_index("c")
    lat = lax.axis_index(LAT)

    @pl.when(band == 0)
    def _():
        copies = [
            pltpu.make_async_copy(above_ref, mid_ref.at[:, 0:3], sems.at[8]),
            pltpu.make_async_copy(tokens_ref, mid_ref.at[:, 3:27], sems.at[9]),
            pltpu.make_async_copy(below_ref, mid_ref.at[:, 27:30], sems.at[10]),
            pltpu.make_async_copy(sibling_ref.at[:, 4:6], inner_ref, sems.at[11]),
        ]
        for n in range(4):
            own = own_qkv_ref.at[:, n] if n < 3 else own_rest_ref.at[:, 0]
            copies.append(pltpu.make_async_copy(own, weights.at[n, :, core], sems.at[n]))
            copies.append(pltpu.make_async_copy(sibling_ref.at[:, n], weights.at[n, :, 1 - core], sems.at[4 + n]))
        for copy in copies:
            copy.start()
        for copy in copies:
            copy.wait()

    gain = gain_ref[...]
    raw = mid_ref[:, pl.ds(band * WL, WL)].reshape(288, 512)
    centre = norm(raw.astype(f32), gain).astype(bf16)
    centre = dot(perm_ref[...], centre)
    outer = norm(outer_ref[...].reshape(72, 512).astype(f32), gain)
    inner = inner_ref.reshape(32, 16, 512)[pl.ds(band * 5, 5)].reshape(80, 512)
    inner = norm(inner.astype(f32)[:72], gain)
    left = jnp.where(core == 0, outer, inner)
    right = jnp.where(core == 0, inner, outer)
    tokens = jnp.concatenate([left, centre, right], axis=0).astype(bf16)
    columns = [weights[n].reshape(512, 512) for n in range(4)]
    q = dot(centre.astype(bf16), columns[0]).astype(bf16) * jnp.asarray(0.125, bf16)
    k = dot(tokens, columns[1]).astype(bf16)
    v = dot(tokens, columns[2]).astype(bf16)
    low = lax.broadcasted_iota(jnp.int32, (1, 128), 1) < 64
    last = lax.axis_size(LAT) - 1
    edge = ((lat == 0) & (band == 0)) | ((lat == last) & (band == bands - 1))
    mask = mask_ref[...] * jnp.where(edge, 1.0, 0.0).astype(f32)
    spans = ((0, 72, 0), (72, 216, 144), (216, 288, 288))
    att = [attend(q[a:b], k[c:c + 144], v[c:c + 144], mask[a:b], low) for a, b, c in spans]
    att = jnp.concatenate(att, axis=0).astype(bf16)
    att = dot(back_ref[...], att).astype(bf16)
    out = dot(att, columns[3]) + raw.astype(f32)
    out = out.astype(bf16).reshape(2, WL, 24, 512)

    @pl.when(band > 0)
    def _():
        fine_ref[:, pl.ds(band * WL - 3, 3)] = out[:, :3]

    @pl.when(band < bands - 1)
    def _():
        fine_ref[:, pl.ds(band * WL, 3)] = out[:, 3:]

    @pl.when(band == bands - 1)
    def _():
        merge_norm(fine_ref, merge_gain_ref, sel_ref, merged_ref)


def merge_kernel(merged_ref, near_ref, far_ref, sibling_near_ref, sibling_far_ref, coarse_ref, weights, sems):
    core = lax.axis_index("c")
    slots = x_slots(lax.axis_index("x"))
    copies = []
    for n, (mine, other) in enumerate(((near_ref, sibling_near_ref), (far_ref, sibling_far_ref))):
        for slot in range(2):
            for col in range(2):
                for m, (ref, at) in enumerate(((mine, core), (other, 1 - core))):
                    copies.append(pltpu.make_async_copy(
                        ref.at[slot, :, col], weights.at[col, :, at, slots[n][slot]], sems.at[((n * 2 + slot) * 2 + col) * 2 + m]))
    for copy in copies:
        copy.start()
    for copy in copies:
        copy.wait()
    for col in range(2):
        part = dot(merged_ref[...], weights[col].reshape(2048, 512))
        coarse_ref[:, col * 512:col * 512 + 512] = part.astype(bf16)


def whole(shape):
    return pl.BlockSpec(shape, lambda *_: (0,) * len(shape))


def pack(w_qkv, w_proj, w_merge):
    return pl.pallas_call(
        pack_kernel,
        in_specs=[VMEM] * 3,
        out_specs=VMEM,
        out_shape=jax.ShapeDtypeStruct((6, 16, 512), bf16),
        name="pack_weights",
    )(w_qkv, w_proj, w_merge)


def edges(tokens, above, below):
    shapes = jax.ShapeDtypeStruct((5, 72, 512), bf16), jax.ShapeDtypeStruct((32, 16, 512), bf16)
    return pl.pallas_call(
        edge_kernel,
        in_specs=[VMEM] * 3,
        out_specs=(VMEM, VMEM),
        out_shape=shapes,
        compiler_params=pltpu.CompilerParams(vmem_limit_bytes=32 << 20),
        cost_estimate=pl.CostEstimate(flops=212_000_000, bytes_accessed=3 << 20, transcendentals=0),
        name="edge_rows",
    )(tokens, above, below)


def attention_block(tokens, above, below, outer, gain, own_qkv, own_rest, sibling, merge_gain):
    perm = one_hot(centre_order(), 288)
    return pl.pallas_call(
        block_kernel,
        grid=(5,),
        in_specs=[
            ANY,
            ANY,
            ANY,
            pl.BlockSpec((1, 72, 512), lambda b: (b, 0, 0)),
            whole((1, 512)),
            ANY,
            ANY,
            ANY,
            whole((288, 288)),
            whole((288, 288)),
            whole((288, 144)),
            whole((1, 2048)),
            whole((288, 288)),
        ],
        out_specs=(whole((2, 24, 24, 512)), whole((288, 2048))),
        out_shape=(jax.ShapeDtypeStruct((2, 24, 24, 512), bf16), jax.ShapeDtypeStruct((288, 2048), bf16)),
        scratch_shapes=[
            pltpu.VMEM((2, 30, 24, 512), bf16),
            pltpu.VMEM((16, 2, 16, 512), bf16),
            pltpu.VMEM((4, 16, 2, 16, 512), bf16),
            pltpu.SemaphoreType.DMA((12,)),
        ],
        compiler_params=pltpu.CompilerParams(vmem_limit_bytes=48 << 20),
        cost_estimate=pl.CostEstimate(flops=5_500_000_000, bytes_accessed=8 << 20, transcendentals=2_500_000),
        name="attention_block",
    )(tokens, above, below, outer, gain.reshape(1, 512), own_qkv, own_rest, sibling,
      jnp.asarray(perm), jnp.asarray(perm.T), jnp.asarray(edge_mask()), merge_gain.reshape(1, 2048),
      jnp.asarray(one_hot(merge_order(), 288)))


def merge_block(merged, near, far, sibling_near, sibling_far):
    return pl.pallas_call(
        merge_kernel,
        in_specs=[VMEM] + [ANY] * 4,
        out_specs=VMEM,
        out_shape=jax.ShapeDtypeStruct((288, 1024), bf16),
        scratch_shapes=[pltpu.VMEM((2, 16, 2, 4, 16, 512), bf16), pltpu.SemaphoreType.DMA((16,))],
        compiler_params=pltpu.CompilerParams(vmem_limit_bytes=40 << 20),
        cost_estimate=pl.CostEstimate(flops=1_200_000_000, bytes_accessed=8 << 20, transcendentals=0),
        name="merge_block",
    )(merged, near, far, sibling_near, sibling_far)


def shift(block, axes, distance):
    devices = range(lax.axis_size(axes))
    route = [((i - distance) % len(devices), i) for i in devices]
    return lax.ppermute(block, axes, route)


def swap(block, axis, partner):
    return lax.ppermute(block, axis, list(enumerate(partner)))


def between_chips(block):
    devices = range(lax.axis_size(LON))
    return lax.ppermute(block, LON, [(i, (i + (1 if i % 2 else -1)) % len(devices)) for i in devices])


def together(*arrays):
    return lax.optimization_barrier(arrays)


def on_device(tokens, attn_gain, w_qkv, w_proj, merge_gain, w_merge):
    above = shift(tokens[:, -3:], LAT, 1)
    below = shift(tokens[:, :3], LAT, -1)
    packed = lax.all_gather(pack(w_qkv, w_proj, w_merge), "zh")
    packed, above, below = together(packed, above, below)
    outer, inner = edges(tokens, above, below)
    outer = between_chips(outer)
    rest = lax.all_gather(packed[:, 3:], "y").reshape(16, 3, 16, 512)
    rest, outer = together(rest, outer)
    first, second = (1, 0, 3, 2), (3, 2, 1, 0)
    merge_own = rest[:, 1:]
    merge_pair = swap(merge_own, "x", first)
    qkv = lax.all_gather(packed[:, :3], "y").reshape(16, 3, 16, 512)
    merge_pair, qkv = together(merge_pair, qkv)
    near = jnp.stack([merge_own, merge_pair])
    far = swap(near, "x", second)
    sibling = shift(jnp.concatenate([qkv, rest[:, :1], inner.reshape(16, 2, 16, 512)], axis=1), "c", 1)
    sibling_near = shift(near, "c", 1)
    fine, merged = attention_block(tokens, above, below, outer, attn_gain, qkv, rest, sibling, merge_gain)
    far, sibling_near, merged = together(far, sibling_near, merged)
    sibling_far = shift(far, "c", 1)
    coarse = merge_block(merged, near, far, sibling_near, sibling_far)
    return fine, coarse.reshape(2, 12, 12, 1024)


def solution(mesh):
    lat, lon = mesh.shape["lat"], mesh.shape["lon"]
    fine_mesh = Mesh(mesh.devices.reshape(lat // 4, 4, 4, lon // 8, 2), LAT + LON)
    in_specs = (P(None, LAT, LON, None), P(), P(LON, None), P(LON, None), P(), P(LON, None))
    out_specs = (P(None, LAT, LON, None), P(None, LAT, LON, None))
    return jax.shard_map(
        on_device, mesh=fine_mesh, in_specs=in_specs, out_specs=out_specs, check_vma=False
    )
```

```python
import numpy as np
import jax
import jax.numpy as jnp
from jax import lax
from jax.sharding import Mesh, PartitionSpec as P
from jax.experimental import pallas as pl
from jax.experimental.pallas import tpu as pltpu

HEADS = 8
WL = 6
eps = 1e-05
f32 = jnp.float32
bf16 = jnp.bfloat16
LAT = ("zl", "x")
LON = ("y", "zh", "c")
VMEM = pl.BlockSpec(memory_space=pltpu.VMEM)
ANY = pl.BlockSpec(memory_space=pl.ANY)


def centre_order():
    return np.array([r * 24 + c for first, last in ((0, 6), (6, 18), (18, 24)) for r in range(4) for c in range(first, last)])


def one_hot(order, n):
    return (order[:, None] == np.arange(n)[None, :]).astype(jnp.bfloat16)


def row_half():
    side = [r // 3 for l in range(2) for r in range(6) for c in range(6)]
    mid = [r // 3 for l in range(2) for r in range(6) for c in range(12)]
    return np.array(side + side + mid + side + side, np.float32)


def edge_mask():
    half = row_half()
    spans = ((0, 72), (72, 216), (216, 288))
    return np.concatenate([
        np.where(half[72 + a:72 + b, None] == half[None, n * 144:n * 144 + 144], 0.0, -1e30).astype(np.float32)
        for n, (a, b) in enumerate(spans)])


def merge_order():
    return np.array([(l * 4 + i) * 24 + 2 * j + p for p in range(2) for i in range(4) for j in range(12) for l in range(2)])


def dot(a, b, ca=1, cb=0):
    return lax.dot_general(a, b, (((ca,), (cb,)), ((), ())), preferred_element_type=f32)


def norm(x, gain):
    centred = x - jnp.mean(x, axis=-1, keepdims=True)
    spread = jnp.mean(centred * centred, axis=-1, keepdims=True)
    return centred * lax.rsqrt(spread + eps) * gain


def pack_kernel(tokens_ref, qkv_ref, proj_ref, merge_ref, out_ref, top_ref, bottom_ref):
    top_ref[...] = tokens_ref[:, 0:3]
    bottom_ref[...] = tokens_ref[:, 21:24]
    for n in range(3):
        out_ref[n] = qkv_ref[:, n * 512:n * 512 + 512]
    out_ref[3] = proj_ref[...]
    quarter = merge_ref[pl.ds(pl.multiple_of(lax.axis_index("x") * 16, 16), 16), :]
    out_ref[4] = quarter[:, :512]
    out_ref[5] = quarter[:, 512:]


def edge_kernel(tokens_ref, above_ref, below_ref, outer_ref, inner_ref):
    first = lax.axis_index("c") == 0
    o = lax.broadcasted_iota(jnp.int32, (144, 288), 0)
    side = (o * 911) >> 16
    lr = ((o - side * 72) * 10923) >> 16
    col = o - side * 72 - lr * 6 + side * 18
    sel = jnp.where(lax.broadcasted_iota(jnp.int32, (144, 288), 1) == lr * 24 + col, 1.0, 0.0).astype(bf16)
    for band in range(5):
        upper = tokens_ref[:, band * WL - 3:band * WL] if band > 0 else above_ref[...]
        lower = tokens_ref[:, band * WL:band * WL + 3] if band < 4 else below_ref[...]
        rows = jnp.concatenate([upper, lower], axis=1).reshape(288, 512)
        both = dot(sel, rows)
        left, right = both[:72], both[72:]
        outer_ref[band] = jnp.where(first, left, right).astype(bf16)
        inner = jnp.concatenate([jnp.where(first, right, left), jnp.zeros((8, 512), f32)], axis=0)
        inner_ref[band * 5:band * 5 + 5] = inner.astype(bf16).reshape(5, 16, 512)
    inner_ref[25:] = jnp.zeros((7, 16, 512), bf16)


def attend(q, k, v, bias, low):
    n = q.shape[0]
    out = []
    ones = jnp.ones((k.shape[0], 128), bf16)
    zero = jnp.zeros((), bf16)
    for pair in range(HEADS // 2):
        cols = slice(pair * 128, pair * 128 + 128)
        qp = q[:, cols]
        both = jnp.concatenate([jnp.where(low, qp, zero), jnp.where(low, zero, qp)], axis=0)
        s = dot(both, k[:, cols], 1, 1)
        s = s + jnp.concatenate([bias, bias], axis=0)
        e = jnp.exp(s - jnp.max(s, axis=-1, keepdims=True)).astype(bf16)
        o = dot(e, jnp.concatenate([v[:, cols], ones], axis=1))
        o = o[:, :128] / o[:, 128:]
        out.append(jnp.where(low, o[:n], o[n:]))
    return jnp.concatenate(out, axis=1)


def merge_norm(fine_ref, gain_ref, sel_ref, merged_ref):
    for chunk in range(3):
        parts = {}
        for p in range(2):
            rows = [fine_ref[l, 2 * (chunk * 4 + i) + p] for l in range(2) for i in range(4)]
            both = dot(sel_ref[...], jnp.concatenate(rows, axis=0))
            parts[p, 0] = both[:96]
            parts[p, 1] = both[96:]
        order = [parts[0, 0], parts[1, 0], parts[0, 1], parts[1, 1]]
        mean = sum(jnp.sum(a, axis=-1, keepdims=True) for a in order) * (1 / 2048)
        centred = [a - mean for a in order]
        spread = sum(jnp.sum(a * a, axis=-1, keepdims=True) for a in centred) * (1 / 2048)
        scale = lax.rsqrt(spread + eps)
        for n, a in enumerate(centred):
            cols = slice(n * 512, n * 512 + 512)
            merged_ref[chunk * 96:chunk * 96 + 96, cols] = (a * scale * gain_ref[:, cols]).astype(bf16)


def block_kernel(tokens_ref, above_ref, below_ref, outer_ref, gain_ref, own_qkv_ref, own_rest_ref, sibling_ref,
                 perm_ref, back_ref, mask_ref, merge_gain_ref, sel_ref, fine_ref, merged_ref,
                 mid_ref, inner_ref, weights, all_ref, q_ref, k_ref, v_ref, att_ref, sems):
    core = lax.axis_index("c")
    lat = lax.axis_index(LAT)
    last = lax.axis_size(LAT) - 1
    bands = 5
    copies = [
        pltpu.make_async_copy(above_ref, mid_ref.at[:, 0:3], sems.at[8]),
        pltpu.make_async_copy(tokens_ref, mid_ref.at[:, 3:27], sems.at[9]),
        pltpu.make_async_copy(below_ref, mid_ref.at[:, 27:30], sems.at[10]),
        pltpu.make_async_copy(sibling_ref.at[:, 4:6], inner_ref, sems.at[11]),
    ]
    for n in range(4):
        own = own_qkv_ref.at[:, n] if n < 3 else own_rest_ref.at[:, 0]
        copies.append(pltpu.make_async_copy(own, weights.at[n, :, core], sems.at[n]))
        copies.append(pltpu.make_async_copy(sibling_ref.at[:, n], weights.at[n, :, 1 - core], sems.at[4 + n]))
    for copy in copies:
        copy.start()
    for copy in copies[:4]:
        copy.wait()
    gain = gain_ref[...]

    def prepare(band, _):
        raw = mid_ref[:, pl.ds(band * WL, WL)].reshape(288, 512)
        centre = norm(raw.astype(f32), gain).astype(bf16)
        sets = [dot(perm_ref[...], centre[n * 96:n * 96 + 96]) for n in range(3)]
        outer = norm(outer_ref[band].astype(f32), gain)
        inner = inner_ref.reshape(32, 16, 512)[pl.ds(band * 5, 5)].reshape(80, 512)
        inner = norm(inner.astype(f32)[:72], gain)
        left = jnp.where(core == 0, outer, inner)
        right = jnp.where(core == 0, inner, outer)
        centre = [part[a:b] for a, b in ((0, 24), (24, 72), (72, 96)) for part in sets]
        rows = jnp.concatenate([left] + centre + [right], axis=0).astype(bf16)
        all_ref[pl.ds(pl.multiple_of(band * 432, 16), 432)] = rows
        return 0

    lax.fori_loop(0, bands, prepare, 0)
    for copy in copies[4:]:
        copy.wait()

    def product(n):
        return dot(all_ref[...], weights[n].reshape(512, 512)).astype(bf16)

    q_ref[...] = product(0) * jnp.asarray(0.125, bf16)
    k_ref[...] = product(1)
    v_ref[...] = product(2)
    low = lax.broadcasted_iota(jnp.int32, (1, 128), 1) < 64

    def attention(band, _):
        rows = pl.ds(pl.multiple_of(band * 432, 16), 432)
        q = q_ref[rows].astype(f32)[72:360].astype(bf16)
        k, v = k_ref[rows], v_ref[rows]
        edge = ((lat == 0) & (band == 0)) | ((lat == last) & (band == bands - 1))
        mask = mask_ref[...] * jnp.where(edge, 1.0, 0.0).astype(f32)
        spans = ((0, 72, 0), (72, 216, 144), (216, 288, 288))
        att = [attend(q[a:b], k[c:c + 144], v[c:c + 144], mask[a:b], low) for a, b, c in spans]
        for n in range(3):
            part = [att[0][24 * n:24 * n + 24], att[1][48 * n:48 * n + 48], att[2][24 * n:24 * n + 24]]
            part = dot(back_ref[...], jnp.concatenate(part, axis=0).astype(bf16)).astype(bf16)
            att_ref[pl.ds(pl.multiple_of(band * 288 + n * 96, 16), 96)] = part
        return 0

    lax.fori_loop(0, bands, attention, 0)
    for band in range(bands):
        raw = mid_ref[:, band * WL:band * WL + WL].reshape(288, 512)
        out = dot(att_ref[band * 288:band * 288 + 288], weights[3].reshape(512, 512)) + raw.astype(f32)
        out = out.astype(bf16).reshape(2, WL, 24, 512)
        if band > 0:
            fine_ref[:, band * WL - 3:band * WL] = out[:, :3]
        if band < bands - 1:
            fine_ref[:, band * WL:band * WL + 3] = out[:, 3:]
    merge_norm(fine_ref, merge_gain_ref, sel_ref, merged_ref)


def merge_kernel(merged_ref, own_ref, pair_ref, across_ref, opposite_ref, sibling_ref, sibling_opposite_ref, coarse_ref,
                 weights, sems):
    core = lax.axis_index("c")
    x = lax.axis_index("x")
    pair = x + 1 - 2 * lax.rem(x, 2)
    pieces = [
        (own_ref.at[:, 1:3], core, x),
        (pair_ref, core, pair),
        (across_ref, core, 3 - x),
        (opposite_ref, core, 3 - pair),
        (sibling_ref.at[0], 1 - core, x),
        (sibling_ref.at[1], 1 - core, pair),
        (sibling_ref.at[2], 1 - core, 3 - x),
        (sibling_opposite_ref, 1 - core, 3 - pair),
    ]
    copies = [pltpu.make_async_copy(ref.at[:, col], weights.at[col, :, at, there], sems.at[2 * n + col])
              for n, (ref, at, there) in enumerate(pieces) for col in range(2)]
    for copy in copies:
        copy.start()
    for copy in copies:
        copy.wait()
    for col in range(2):
        part = dot(merged_ref[...], weights[col].reshape(2048, 512)).astype(bf16)
        coarse_ref[:, :, col * 512:col * 512 + 512] = part.reshape(144, 2, 512)


def pack(tokens, w_qkv, w_proj, w_merge):
    rows = jax.ShapeDtypeStruct((2, 3, 24, 512), bf16)
    return pl.pallas_call(
        pack_kernel,
        in_specs=[VMEM] * 4,
        out_specs=(VMEM,) * 3,
        out_shape=(jax.ShapeDtypeStruct((6, 16, 512), bf16), rows, rows),
        name="pack_parts",
    )(tokens, w_qkv, w_proj, w_merge)


def edges(tokens, above, below):
    shapes = jax.ShapeDtypeStruct((5, 72, 512), bf16), jax.ShapeDtypeStruct((32, 16, 512), bf16)
    return pl.pallas_call(
        edge_kernel,
        in_specs=[VMEM] * 3,
        out_specs=(VMEM, VMEM),
        out_shape=shapes,
        compiler_params=pltpu.CompilerParams(vmem_limit_bytes=32 << 20),
        cost_estimate=pl.CostEstimate(flops=212_000_000, bytes_accessed=3 << 20, transcendentals=0),
        name="edge_rows",
    )(tokens, above, below)


def attention_block(tokens, above, below, outer, gain, own_qkv, own_rest, sibling, merge_gain):
    perm = one_hot(centre_order(), 96)
    return pl.pallas_call(
        block_kernel,
        in_specs=[ANY, ANY, ANY, VMEM, VMEM, ANY, ANY, ANY] + [VMEM] * 5,
        out_specs=(VMEM, VMEM),
        out_shape=(jax.ShapeDtypeStruct((2, 24, 24, 512), bf16), jax.ShapeDtypeStruct((288, 2048), bf16)),
        scratch_shapes=[
            pltpu.VMEM((2, 30, 24, 512), bf16),
            pltpu.VMEM((16, 2, 16, 512), bf16),
            pltpu.VMEM((4, 16, 2, 16, 512), bf16),
            pltpu.VMEM((2160, 512), bf16),
            pltpu.VMEM((2160, 512), bf16),
            pltpu.VMEM((2160, 512), bf16),
            pltpu.VMEM((2160, 512), bf16),
            pltpu.VMEM((1440, 512), bf16),
            pltpu.SemaphoreType.DMA((12,)),
        ],
        compiler_params=pltpu.CompilerParams(vmem_limit_bytes=40 << 20),
        cost_estimate=pl.CostEstimate(flops=5_500_000_000, bytes_accessed=8 << 20, transcendentals=2_500_000),
        name="attention_block",
    )(tokens, above, below, outer, gain.reshape(1, 512), own_qkv, own_rest, sibling,
      jnp.asarray(perm), jnp.asarray(perm.T), jnp.asarray(edge_mask()), merge_gain.reshape(1, 2048),
      jnp.asarray(one_hot(merge_order(), 192)))


def merge_block(merged, own, pair, across, opposite, sibling, sibling_opposite):
    return pl.pallas_call(
        merge_kernel,
        in_specs=[VMEM] + [ANY] * 6,
        out_specs=VMEM,
        out_shape=jax.ShapeDtypeStruct((144, 2, 1024), bf16),
        scratch_shapes=[pltpu.VMEM((2, 16, 2, 4, 16, 512), bf16), pltpu.SemaphoreType.DMA((16,))],
        compiler_params=pltpu.CompilerParams(vmem_limit_bytes=24 << 20),
        cost_estimate=pl.CostEstimate(flops=1_200_000_000, bytes_accessed=8 << 20, transcendentals=0),
        name="merge_block",
    )(merged, own, pair, across, opposite, sibling, sibling_opposite)


def shift(block, axes, distance):
    devices = range(lax.axis_size(axes))
    route = [((i - distance) % len(devices), i) for i in devices]
    return lax.ppermute(block, axes, route)


def swap(block, axis, partner):
    return lax.ppermute(block, axis, list(enumerate(partner)))


def between_chips(block):
    devices = range(lax.axis_size(LON))
    return lax.ppermute(block, LON, [(i, (i + (1 if i % 2 else -1)) % len(devices)) for i in devices])


def together(*arrays):
    return lax.optimization_barrier(arrays)


def on_device(tokens, attn_gain, w_qkv, w_proj, merge_gain, w_merge):
    packed, top, bottom = pack(tokens, w_qkv, w_proj, w_merge)
    above = shift(bottom, LAT, 1)
    below = shift(top, LAT, -1)
    packed = lax.all_gather(packed, "zh")
    packed, above, below = together(packed, above, below)
    outer, inner = edges(tokens, above, below)
    outer = between_chips(outer)
    rest = lax.all_gather(packed[:, 3:], "y").reshape(16, 3, 16, 512)
    first, second = (1, 0, 3, 2), (3, 2, 1, 0)
    merge_own = rest[:, 1:]
    pair = swap(merge_own, "x", first)
    across = swap(merge_own, "x", second)
    qkv = lax.all_gather(packed[:, :3], "y").reshape(16, 3, 16, 512)
    pair, across, qkv, outer = together(pair, across, qkv, outer)
    opposite = swap(across, "x", first)
    sibling = shift(jnp.concatenate([qkv, rest[:, :1], inner.reshape(16, 2, 16, 512)], axis=1), "c", 1)
    sibling_merge = shift(jnp.stack([merge_own, pair, across]), "c", 1)
    fine, merged = attention_block(tokens, above, below, outer, attn_gain, qkv, rest, sibling, merge_gain)
    opposite, sibling_merge, merged = together(opposite, sibling_merge, merged)
    sibling_opposite = shift(opposite, "c", 1)
    coarse = merge_block(merged, rest, pair, across, opposite, sibling_merge, sibling_opposite)
    return fine, coarse.reshape(12, 12, 2, 1024).transpose(2, 0, 1, 3)


def solution(mesh):
    lat, lon = mesh.shape["lat"], mesh.shape["lon"]
    fine_mesh = Mesh(mesh.devices.reshape(lat // 4, 4, 4, lon // 8, 2), LAT + LON)
    in_specs = (P(None, LAT, LON, None), P(), P(LON, None), P(LON, None), P(), P(LON, None))
    out_specs = (P(None, LAT, LON, None), P(None, LAT, LON, None))
    return jax.shard_map(
        on_device, mesh=fine_mesh, in_specs=in_specs, out_specs=out_specs, check_vma=False
    )
```

```python
import numpy as np
import jax
import jax.numpy as jnp
from jax import lax
from jax.sharding import Mesh, PartitionSpec as P
from jax.experimental import pallas as pl
from jax.experimental.pallas import tpu as pltpu

HEADS = 8
WL = 6
eps = 1e-05
f32 = jnp.float32
bf16 = jnp.bfloat16
LAT = ("zl", "x")
LON = ("y", "zh", "c")
VMEM = pl.BlockSpec(memory_space=pltpu.VMEM)
ANY = pl.BlockSpec(memory_space=pl.ANY)


def centre_order():
    return np.array([r * 24 + c for first, last in ((0, 6), (6, 18), (18, 24)) for r in range(4) for c in range(first, last)])


def one_hot(order, n):
    return (order[:, None] == np.arange(n)[None, :]).astype(jnp.bfloat16)


def row_half():
    side = [r // 3 for l in range(2) for r in range(6) for c in range(6)]
    mid = [r // 3 for l in range(2) for r in range(6) for c in range(12)]
    return np.array(side + side + mid + side + side, np.float32)


def edge_mask():
    half = row_half()
    spans = ((0, 72), (72, 216), (216, 288))
    return np.concatenate([
        np.where(half[72 + a:72 + b, None] == half[None, n * 144:n * 144 + 144], 0.0, -1e30).astype(np.float32)
        for n, (a, b) in enumerate(spans)])


def merge_order():
    return np.array([(l * 4 + i) * 24 + 2 * j + p for p in range(2) for i in range(4) for j in range(12) for l in range(2)])


def dot(a, b, ca=1, cb=0):
    return lax.dot_general(a, b, (((ca,), (cb,)), ((), ())), preferred_element_type=f32)


def norm(x, gain):
    centred = x - jnp.mean(x, axis=-1, keepdims=True)
    spread = jnp.mean(centred * centred, axis=-1, keepdims=True)
    return centred * lax.rsqrt(spread + eps) * gain


def pack_kernel(tokens_ref, qkv_ref, proj_ref, merge_ref, out_ref, top_ref, bottom_ref):
    top_ref[...] = tokens_ref[:, 0:3]
    bottom_ref[...] = tokens_ref[:, 21:24]
    for n in range(3):
        out_ref[n] = qkv_ref[:, n * 512:n * 512 + 512]
    out_ref[3] = proj_ref[...]
    quarter = merge_ref[pl.ds(pl.multiple_of(lax.axis_index("x") * 16, 16), 16), :]
    out_ref[4] = quarter[:, :512]
    out_ref[5] = quarter[:, 512:]


def edge_kernel(tokens_ref, above_ref, below_ref, outer_ref, inner_ref):
    first = lax.axis_index("c") == 0
    o = lax.broadcasted_iota(jnp.int32, (144, 288), 0)
    side = (o * 911) >> 16
    lr = ((o - side * 72) * 10923) >> 16
    col = o - side * 72 - lr * 6 + side * 18
    sel = jnp.where(lax.broadcasted_iota(jnp.int32, (144, 288), 1) == lr * 24 + col, 1.0, 0.0).astype(bf16)
    for band in range(5):
        upper = tokens_ref[:, band * WL - 3:band * WL] if band > 0 else above_ref[...]
        lower = tokens_ref[:, band * WL:band * WL + 3] if band < 4 else below_ref[...]
        rows = jnp.concatenate([upper, lower], axis=1).reshape(288, 512)
        both = dot(sel, rows)
        left, right = both[:72], both[72:]
        outer_ref[band] = jnp.where(first, left, right).astype(bf16)
        inner = jnp.concatenate([jnp.where(first, right, left), jnp.zeros((8, 512), f32)], axis=0)
        inner_ref[band * 5:band * 5 + 5] = inner.astype(bf16).reshape(5, 16, 512)
    inner_ref[25:] = jnp.zeros((7, 16, 512), bf16)


def attend(q, k, v, bias, low):
    n = q.shape[0]
    out = []
    ones = jnp.ones((k.shape[0], 128), bf16)
    zero = jnp.zeros((), bf16)
    for pair in range(HEADS // 2):
        cols = slice(pair * 128, pair * 128 + 128)
        qp = q[:, cols]
        both = jnp.concatenate([jnp.where(low, qp, zero), jnp.where(low, zero, qp)], axis=0)
        s = dot(both, k[:, cols], 1, 1)
        if bias is not None:
            s = s + jnp.concatenate([bias, bias], axis=0)
        e = jnp.exp(s - jnp.max(s, axis=-1, keepdims=True)).astype(bf16)
        o = dot(e, jnp.concatenate([v[:, cols], ones], axis=1))
        o = o[:, :128] / o[:, 128:]
        out.append(jnp.where(low, o[:n], o[n:]))
    return jnp.concatenate(out, axis=1)


def merge_norm(fine_ref, gain_ref, sel_ref, merged_ref):
    for chunk in range(3):
        parts = {}
        for p in range(2):
            rows = [fine_ref[l, 2 * (chunk * 4 + i) + p] for l in range(2) for i in range(4)]
            both = dot(sel_ref[...], jnp.concatenate(rows, axis=0))
            parts[p, 0] = both[:96]
            parts[p, 1] = both[96:]
        order = [parts[0, 0], parts[1, 0], parts[0, 1], parts[1, 1]]
        mean = sum(jnp.sum(a, axis=-1, keepdims=True) for a in order) * (1 / 2048)
        centred = [a - mean for a in order]
        spread = sum(jnp.sum(a * a, axis=-1, keepdims=True) for a in centred) * (1 / 2048)
        scale = lax.rsqrt(spread + eps)
        for n, a in enumerate(centred):
            cols = slice(n * 512, n * 512 + 512)
            merged_ref[chunk * 96:chunk * 96 + 96, cols] = (a * scale * gain_ref[:, cols]).astype(bf16)


def block_kernel(tokens_ref, above_ref, below_ref, outer_ref, gain_ref, own_qkv_ref, own_rest_ref, sibling_ref,
                 perm_ref, back_ref, mask_ref, merge_gain_ref, sel_ref, result_ref, merged_ref,
                 fine_ref, mid_ref, inner_ref, weights, sems):
    core = lax.axis_index("c")
    lat = lax.axis_index(LAT)
    last = lax.axis_size(LAT) - 1
    bands = 5
    copies = [
        pltpu.make_async_copy(above_ref, mid_ref.at[:, 0:3], sems.at[8]),
        pltpu.make_async_copy(tokens_ref, mid_ref.at[:, 3:27], sems.at[9]),
        pltpu.make_async_copy(below_ref, mid_ref.at[:, 27:30], sems.at[10]),
        pltpu.make_async_copy(sibling_ref.at[:, 4:6], inner_ref, sems.at[11]),
    ]
    for n in range(4):
        own = own_qkv_ref.at[:, n] if n < 3 else own_rest_ref.at[:, 0]
        copies.append(pltpu.make_async_copy(own, weights.at[n, :, core], sems.at[n]))
        copies.append(pltpu.make_async_copy(sibling_ref.at[:, n], weights.at[n, :, 1 - core], sems.at[4 + n]))
    for copy in copies:
        copy.start()
    for copy in copies[:4]:
        copy.wait()
    gain = gain_ref[...]

    low = lax.broadcasted_iota(jnp.int32, (1, 128), 1) < 64
    def prepare(band):
        raw = mid_ref[:, band * WL:band * WL + WL].reshape(288, 512)
        centre = norm(raw.astype(f32), gain).astype(bf16)
        sets = [dot(perm_ref[...], centre[n * 96:n * 96 + 96]) for n in range(3)]
        outer = norm(outer_ref[band].astype(f32), gain)
        inner = inner_ref.reshape(32, 16, 512)[band * 5:band * 5 + 5].reshape(80, 512)
        inner = norm(inner.astype(f32)[:72], gain)
        left = jnp.where(core == 0, outer, inner)
        right = jnp.where(core == 0, inner, outer)
        centre = [part[a:b] for a, b in ((0, 24), (24, 72), (72, 96)) for part in sets]
        rows = jnp.concatenate([left] + centre + [right], axis=0).astype(bf16)
        return rows, jnp.concatenate(centre, axis=0).astype(bf16)

    def attention(band, q, k, v):
        mask = [None] * 3
        spans = ((0, 72, 0), (72, 216, 144), (216, 288, 288))
        if band in (0, bands - 1):
            edge = (lat == 0) if band == 0 else (lat == last)
            bias = mask_ref[...] * jnp.where(edge, 1.0, 0.0).astype(f32)
            mask = [bias[a:b] for a, b, c in spans]
        att = [attend(q[a:b], k[c:c + 144], v[c:c + 144], m, low) for (a, b, c), m in zip(spans, mask)]
        parts = []
        for n in range(3):
            part = [att[0][24 * n:24 * n + 24], att[1][48 * n:48 * n + 48], att[2][24 * n:24 * n + 24]]
            parts.append(dot(back_ref[...], jnp.concatenate(part, axis=0).astype(bf16)))
        return jnp.concatenate(parts, axis=0).astype(bf16)

    def finish(band, part, raw):
        out = dot(part, weights[3].reshape(512, 512)) + raw.astype(f32)
        out = out.astype(bf16).reshape(2, WL, 24, 512)
        if band > 0:
            fine_ref[:, band * WL - 3:band * WL] = out[:, :3]
        if band < bands - 1:
            fine_ref[:, band * WL:band * WL + 3] = out[:, 3:]
        rows = pl.ds(max(band * WL - 3, 0), 3 if band in (0, bands - 1) else WL)
        copy = pltpu.make_async_copy(fine_ref.at[:, rows], result_ref.at[:, rows], sems.at[12 + band])
        copy.start()
        return copy

    scale = jnp.asarray(0.125, bf16)

    def project(band):
        rows, centre = prepare(band)
        q = dot(centre, weights[0].reshape(512, 512)).astype(bf16) * scale
        k = dot(rows, weights[1].reshape(512, 512)).astype(bf16)
        v = dot(rows, weights[2].reshape(512, 512)).astype(bf16)
        return q, k, v

    for copy in copies[4:]:
        copy.wait()
    copies = []
    held = project(0)
    for band in range(bands):
        following = project(band + 1) if band < bands - 1 else None
        raw = mid_ref[:, band * WL:band * WL + WL].reshape(288, 512)
        copies.append(finish(band, attention(band, *held), raw))
        held = following
    merge_norm(fine_ref, merge_gain_ref, sel_ref, merged_ref)
    for copy in copies:
        copy.wait()


def merge_kernel(merged_ref, own_ref, pair_ref, across_ref, opposite_ref, sibling_ref, sibling_opposite_ref, coarse_ref,
                 weights, sems):
    core = lax.axis_index("c")
    x = lax.axis_index("x")
    pair = x + 1 - 2 * lax.rem(x, 2)
    pieces = [
        (own_ref.at[:, 1:3], core, x),
        (pair_ref, core, pair),
        (across_ref, core, 3 - x),
        (opposite_ref, core, 3 - pair),
        (sibling_ref.at[0], 1 - core, x),
        (sibling_ref.at[1], 1 - core, pair),
        (sibling_ref.at[2], 1 - core, 3 - x),
        (sibling_opposite_ref, 1 - core, 3 - pair),
    ]
    copies = [pltpu.make_async_copy(ref.at[:, col], weights.at[col, :, at, there], sems.at[2 * n + col])
              for col in range(2) for n, (ref, at, there) in enumerate(pieces)]
    for copy in copies:
        copy.start()
    for col in range(2):
        for copy in copies[8 * col:8 * col + 8]:
            copy.wait()
        part = dot(merged_ref[...], weights[col].reshape(2048, 512)).astype(bf16)
        coarse_ref[:, :, col * 512:col * 512 + 512] = part.reshape(144, 2, 512)


def pack(tokens, w_qkv, w_proj, w_merge):
    rows = jax.ShapeDtypeStruct((2, 3, 24, 512), bf16)
    return pl.pallas_call(
        pack_kernel,
        in_specs=[VMEM] * 4,
        out_specs=(VMEM,) * 3,
        out_shape=(jax.ShapeDtypeStruct((6, 16, 512), bf16), rows, rows),
        name="pack_parts",
    )(tokens, w_qkv, w_proj, w_merge)


def edges(tokens, above, below):
    shapes = jax.ShapeDtypeStruct((5, 72, 512), bf16), jax.ShapeDtypeStruct((32, 16, 512), bf16)
    return pl.pallas_call(
        edge_kernel,
        in_specs=[VMEM] * 3,
        out_specs=(VMEM, VMEM),
        out_shape=shapes,
        compiler_params=pltpu.CompilerParams(vmem_limit_bytes=32 << 20),
        cost_estimate=pl.CostEstimate(flops=212_000_000, bytes_accessed=3 << 20, transcendentals=0),
        name="edge_rows",
    )(tokens, above, below)


def attention_block(tokens, above, below, outer, gain, own_qkv, own_rest, sibling, merge_gain):
    perm = one_hot(centre_order(), 96)
    return pl.pallas_call(
        block_kernel,
        in_specs=[ANY, ANY, ANY, VMEM, VMEM, ANY, ANY, ANY] + [VMEM] * 5,
        out_specs=(ANY, VMEM),
        out_shape=(jax.ShapeDtypeStruct((2, 24, 24, 512), bf16), jax.ShapeDtypeStruct((288, 2048), bf16)),
        scratch_shapes=[
            pltpu.VMEM((2, 24, 24, 512), bf16),
            pltpu.VMEM((2, 30, 24, 512), bf16),
            pltpu.VMEM((16, 2, 16, 512), bf16),
            pltpu.VMEM((4, 16, 2, 16, 512), bf16),
            pltpu.SemaphoreType.DMA((17,)),
        ],
        compiler_params=pltpu.CompilerParams(vmem_limit_bytes=40 << 20),
        cost_estimate=pl.CostEstimate(flops=5_500_000_000, bytes_accessed=8 << 20, transcendentals=2_500_000),
        name="attention_block",
    )(tokens, above, below, outer, gain.reshape(1, 512), own_qkv, own_rest, sibling,
      jnp.asarray(perm), jnp.asarray(perm.T), jnp.asarray(edge_mask()), merge_gain.reshape(1, 2048),
      jnp.asarray(one_hot(merge_order(), 192)))


def merge_block(merged, own, pair, across, opposite, sibling, sibling_opposite):
    return pl.pallas_call(
        merge_kernel,
        in_specs=[VMEM] + [ANY] * 6,
        out_specs=VMEM,
        out_shape=jax.ShapeDtypeStruct((144, 2, 1024), bf16),
        scratch_shapes=[pltpu.VMEM((2, 16, 2, 4, 16, 512), bf16), pltpu.SemaphoreType.DMA((16,))],
        compiler_params=pltpu.CompilerParams(vmem_limit_bytes=24 << 20),
        cost_estimate=pl.CostEstimate(flops=1_200_000_000, bytes_accessed=8 << 20, transcendentals=0),
        name="merge_block",
    )(merged, own, pair, across, opposite, sibling, sibling_opposite)


def shift(block, axes, distance):
    devices = range(lax.axis_size(axes))
    route = [((i - distance) % len(devices), i) for i in devices]
    return lax.ppermute(block, axes, route)


def swap(block, axis, partner):
    return lax.ppermute(block, axis, list(enumerate(partner)))


def between_chips(block):
    devices = range(lax.axis_size(LON))
    return lax.ppermute(block, LON, [(i, (i + (1 if i % 2 else -1)) % len(devices)) for i in devices])


def together(*arrays):
    return lax.optimization_barrier(arrays)


def on_device(tokens, attn_gain, w_qkv, w_proj, merge_gain, w_merge):
    packed, top, bottom = pack(tokens, w_qkv, w_proj, w_merge)
    above = shift(bottom, LAT, 1)
    below = shift(top, LAT, -1)
    packed = lax.all_gather(packed, "zh")
    packed, above, below = together(packed, above, below)
    outer, inner = edges(tokens, above, below)
    outer = between_chips(outer)
    rest = lax.all_gather(packed[:, 3:], "y").reshape(16, 3, 16, 512)
    first, second = (1, 0, 3, 2), (3, 2, 1, 0)
    merge_own = rest[:, 1:]
    pair = swap(merge_own, "x", first)
    across = swap(merge_own, "x", second)
    qkv = lax.all_gather(packed[:, :3], "y").reshape(16, 3, 16, 512)
    pair, across, qkv = together(pair, across, qkv)
    across, outer = together(across, outer)
    opposite = swap(across, "x", first)
    sibling = shift(jnp.concatenate([qkv, rest[:, :1], inner.reshape(16, 2, 16, 512)], axis=1), "c", 1)
    sibling_merge = shift(jnp.stack([merge_own, pair, across]), "c", 1)
    fine, merged = attention_block(tokens, above, below, outer, attn_gain, qkv, rest, sibling, merge_gain)
    opposite, sibling_merge, merged = together(opposite, sibling_merge, merged)
    sibling_opposite = shift(opposite, "c", 1)
    coarse = merge_block(merged, rest, pair, across, opposite, sibling_merge, sibling_opposite)
    return fine, coarse.reshape(12, 12, 2, 1024).transpose(2, 0, 1, 3)


def solution(mesh):
    lat, lon = mesh.shape["lat"], mesh.shape["lon"]
    fine_mesh = Mesh(mesh.devices.reshape(lat // 4, 4, 4, lon // 8, 2), LAT + LON)
    in_specs = (P(None, LAT, LON, None), P(), P(LON, None), P(LON, None), P(), P(LON, None))
    out_specs = (P(None, LAT, LON, None), P(None, LAT, LON, None))
    return jax.shard_map(
        on_device, mesh=fine_mesh, in_specs=in_specs, out_specs=out_specs, check_vma=False
    )
```

```python
import numpy as np
import jax
import jax.numpy as jnp
from jax import lax
from jax.sharding import Mesh, PartitionSpec as P
from jax.experimental import pallas as pl
from jax.experimental.pallas import tpu as pltpu

HEADS = 8
WL = 6
eps = 1e-05
f32 = jnp.float32
bf16 = jnp.bfloat16
LAT = ("zl", "x")
LON = ("y", "zh", "c")
VMEM = pl.BlockSpec(memory_space=pltpu.VMEM)
ANY = pl.BlockSpec(memory_space=pl.ANY)


def centre_order():
    return np.array([r * 24 + c for first, last in ((0, 6), (6, 18), (18, 24)) for r in range(4) for c in range(first, last)])


def one_hot(order, n):
    return (order[:, None] == np.arange(n)[None, :]).astype(jnp.bfloat16)


def row_half():
    side = [r // 3 for l in range(2) for r in range(6) for c in range(6)]
    mid = [r // 3 for l in range(2) for r in range(6) for c in range(12)]
    return np.array(side + side + mid + side + side, np.float32)


def edge_mask():
    half = row_half()
    spans = ((0, 72), (72, 216), (216, 288))
    return np.concatenate([
        np.where(half[72 + a:72 + b, None] == half[None, n * 144:n * 144 + 144], 0.0, -1e30).astype(np.float32)
        for n, (a, b) in enumerate(spans)])


def merge_order():
    return np.array([(l * 4 + i) * 24 + 2 * j + p for p in range(2) for i in range(4) for j in range(12) for l in range(2)])


def dot(a, b, ca=1, cb=0):
    return lax.dot_general(a, b, (((ca,), (cb,)), ((), ())), preferred_element_type=f32)


def norm(x, gain):
    centred = x - jnp.mean(x, axis=-1, keepdims=True)
    spread = jnp.mean(centred * centred, axis=-1, keepdims=True)
    return centred * lax.rsqrt(spread + eps) * gain


def pack_kernel(tokens_ref, qkv_ref, proj_ref, merge_ref, out_ref, top_ref, bottom_ref, sems):
    rows = pl.ds(pl.multiple_of(lax.axis_index("x") * 16, 16), 16)
    pairs = [(tokens_ref.at[:, 0:3], top_ref), (tokens_ref.at[:, 21:24], bottom_ref), (proj_ref, out_ref.at[3])]
    pairs += [(qkv_ref.at[:, n * 512:n * 512 + 512], out_ref.at[n]) for n in range(3)]
    pairs += [(merge_ref.at[rows, n * 512:n * 512 + 512], out_ref.at[4 + n]) for n in range(2)]
    copies = [pltpu.make_async_copy(source, target, sems.at[n]) for n, (source, target) in enumerate(pairs)]
    for copy in copies:
        copy.start()
    for copy in copies:
        copy.wait()


def edge_kernel(tokens_ref, above_ref, below_ref, outer_ref, inner_ref):
    first = lax.axis_index("c") == 0
    o = lax.broadcasted_iota(jnp.int32, (144, 288), 0)
    side = (o * 911) >> 16
    lr = ((o - side * 72) * 10923) >> 16
    col = o - side * 72 - lr * 6 + side * 18
    sel = jnp.where(lax.broadcasted_iota(jnp.int32, (144, 288), 1) == lr * 24 + col, 1.0, 0.0).astype(bf16)
    for band in range(5):
        upper = tokens_ref[:, band * WL - 3:band * WL] if band > 0 else above_ref[...]
        lower = tokens_ref[:, band * WL:band * WL + 3] if band < 4 else below_ref[...]
        rows = jnp.concatenate([upper, lower], axis=1).reshape(288, 512)
        both = dot(sel, rows)
        left, right = both[:72], both[72:]
        outer_ref[band] = jnp.where(first, left, right).astype(bf16)
        inner = jnp.concatenate([jnp.where(first, right, left), jnp.zeros((8, 512), f32)], axis=0)
        inner_ref[band * 5:band * 5 + 5] = inner.astype(bf16).reshape(5, 16, 512)
    inner_ref[25:] = jnp.zeros((7, 16, 512), bf16)


def attend(q, k, v, bias, low):
    n = q.shape[0]
    out = []
    ones = jnp.ones((k.shape[0], 128), bf16)
    zero = jnp.zeros((), bf16)
    for pair in range(HEADS // 2):
        cols = slice(pair * 128, pair * 128 + 128)
        qp = q[:, cols]
        both = jnp.concatenate([jnp.where(low, qp, zero), jnp.where(low, zero, qp)], axis=0)
        s = dot(both, k[:, cols], 1, 1)
        if bias is not None:
            s = s + jnp.concatenate([bias, bias], axis=0)
        e = jnp.exp(s - jnp.max(s, axis=-1, keepdims=True)).astype(bf16)
        o = dot(e, jnp.concatenate([v[:, cols], ones], axis=1))
        o = o[:, :128] / o[:, 128:]
        out.append(jnp.where(low, o[:n], o[n:]))
    return jnp.concatenate(out, axis=1)


def merge_norm(fine_ref, gain_ref, sel_ref, merged_ref):
    for chunk in range(3):
        parts = {}
        for p in range(2):
            rows = [fine_ref[l, 2 * (chunk * 4 + i) + p] for l in range(2) for i in range(4)]
            both = dot(sel_ref[...], jnp.concatenate(rows, axis=0))
            parts[p, 0] = both[:96]
            parts[p, 1] = both[96:]
        order = [parts[0, 0], parts[1, 0], parts[0, 1], parts[1, 1]]
        mean = sum(jnp.sum(a, axis=-1, keepdims=True) for a in order) * (1 / 2048)
        centred = [a - mean for a in order]
        spread = sum(jnp.sum(a * a, axis=-1, keepdims=True) for a in centred) * (1 / 2048)
        scale = lax.rsqrt(spread + eps)
        for n, a in enumerate(centred):
            cols = slice(n * 512, n * 512 + 512)
            merged_ref[chunk * 96:chunk * 96 + 96, cols] = (a * scale * gain_ref[:, cols]).astype(bf16)


def block_kernel(tokens_ref, above_ref, below_ref, outer_ref, gain_ref, own_qkv_ref, own_rest_ref, sibling_ref,
                 perm_ref, back_ref, mask_ref, merge_gain_ref, sel_ref, result_ref, merged_ref,
                 fine_ref, mid_ref, inner_ref, weights, sems):
    core = lax.axis_index("c")
    lat = lax.axis_index(LAT)
    last = lax.axis_size(LAT) - 1
    bands = 5
    copies = [
        pltpu.make_async_copy(above_ref, mid_ref.at[:, 0:3], sems.at[8]),
        pltpu.make_async_copy(tokens_ref, mid_ref.at[:, 3:27], sems.at[9]),
        pltpu.make_async_copy(below_ref, mid_ref.at[:, 27:30], sems.at[10]),
        pltpu.make_async_copy(sibling_ref.at[:, 4:6], inner_ref, sems.at[11]),
    ]
    for n in range(4):
        own = own_qkv_ref.at[:, n] if n < 3 else own_rest_ref.at[:, 0]
        copies.append(pltpu.make_async_copy(own, weights.at[n, :, core], sems.at[n]))
        copies.append(pltpu.make_async_copy(sibling_ref.at[:, n], weights.at[n, :, 1 - core], sems.at[4 + n]))
    for copy in copies:
        copy.start()
    for copy in copies[:4]:
        copy.wait()
    gain = gain_ref[...]

    low = lax.broadcasted_iota(jnp.int32, (1, 128), 1) < 64
    def prepare(band):
        raw = mid_ref[:, band * WL:band * WL + WL].reshape(288, 512)
        centre = norm(raw.astype(f32), gain).astype(bf16)
        sets = [dot(perm_ref[...], centre[n * 96:n * 96 + 96]) for n in range(3)]
        outer = norm(outer_ref[band].astype(f32), gain)
        inner = inner_ref.reshape(32, 16, 512)[band * 5:band * 5 + 5].reshape(80, 512)
        inner = norm(inner.astype(f32)[:72], gain)
        left = jnp.where(core == 0, outer, inner)
        right = jnp.where(core == 0, inner, outer)
        centre = [part[a:b] for a, b in ((0, 24), (24, 72), (72, 96)) for part in sets]
        rows = jnp.concatenate([left] + centre + [right], axis=0).astype(bf16)
        return rows, jnp.concatenate(centre, axis=0).astype(bf16)

    def attention(band, q, k, v):
        mask = [None] * 3
        spans = ((0, 72, 0), (72, 216, 144), (216, 288, 288))
        if band in (0, bands - 1):
            edge = (lat == 0) if band == 0 else (lat == last)
            bias = mask_ref[...] * jnp.where(edge, 1.0, 0.0).astype(f32)
            mask = [bias[a:b] for a, b, c in spans]
        att = [attend(q[a:b], k[c:c + 144], v[c:c + 144], m, low) for (a, b, c), m in zip(spans, mask)]
        parts = []
        for n in range(3):
            part = [att[0][24 * n:24 * n + 24], att[1][48 * n:48 * n + 48], att[2][24 * n:24 * n + 24]]
            parts.append(dot(back_ref[...], jnp.concatenate(part, axis=0).astype(bf16)))
        return jnp.concatenate(parts, axis=0).astype(bf16)

    def finish(band, part, raw):
        out = dot(part, weights[3].reshape(512, 512)) + raw.astype(f32)
        out = out.astype(bf16).reshape(2, WL, 24, 512)
        if band > 0:
            fine_ref[:, band * WL - 3:band * WL] = out[:, :3]
        if band < bands - 1:
            fine_ref[:, band * WL:band * WL + 3] = out[:, 3:]
        rows = pl.ds(max(band * WL - 3, 0), 3 if band in (0, bands - 1) else WL)
        copy = pltpu.make_async_copy(fine_ref.at[:, rows], result_ref.at[:, rows], sems.at[12 + band])
        copy.start()
        return copy

    scale = jnp.asarray(0.125, bf16)

    def project(band):
        rows, centre = prepare(band)
        q = dot(centre, weights[0].reshape(512, 512)).astype(bf16) * scale
        k = dot(rows, weights[1].reshape(512, 512)).astype(bf16)
        v = dot(rows, weights[2].reshape(512, 512)).astype(bf16)
        return q, k, v

    for copy in copies[4:]:
        copy.wait()
    copies = []
    held = project(0)
    for band in range(bands):
        following = project(band + 1) if band < bands - 1 else None
        raw = mid_ref[:, band * WL:band * WL + WL].reshape(288, 512)
        copies.append(finish(band, attention(band, *held), raw))
        held = following
    merge_norm(fine_ref, merge_gain_ref, sel_ref, merged_ref)
    for copy in copies:
        copy.wait()


def merge_kernel(merged_ref, own_ref, pair_ref, across_ref, opposite_ref, sibling_ref, sibling_opposite_ref, coarse_ref,
                 weights, sems):
    core = lax.axis_index("c")
    x = lax.axis_index("x")
    pair = x + 1 - 2 * lax.rem(x, 2)
    pieces = [
        (own_ref.at[:, 1:3], core, x),
        (pair_ref, core, pair),
        (across_ref, core, 3 - x),
        (opposite_ref, core, 3 - pair),
        (sibling_ref.at[0], 1 - core, x),
        (sibling_ref.at[1], 1 - core, pair),
        (sibling_ref.at[2], 1 - core, 3 - x),
        (sibling_opposite_ref, 1 - core, 3 - pair),
    ]
    copies = [pltpu.make_async_copy(ref.at[:, col], weights.at[col, :, at, there], sems.at[2 * n + col])
              for col in range(2) for n, (ref, at, there) in enumerate(pieces)]
    for copy in copies:
        copy.start()
    for col in range(2):
        for copy in copies[8 * col:8 * col + 8]:
            copy.wait()
        part = dot(merged_ref[...], weights[col].reshape(2048, 512)).astype(bf16)
        coarse_ref[:, :, col * 512:col * 512 + 512] = part.reshape(144, 2, 512)


def pack(tokens, w_qkv, w_proj, w_merge):
    rows = jax.ShapeDtypeStruct((2, 3, 24, 512), bf16)
    return pl.pallas_call(
        pack_kernel,
        in_specs=[ANY] * 4,
        out_specs=(VMEM,) * 3,
        out_shape=(jax.ShapeDtypeStruct((6, 16, 512), bf16), rows, rows),
        scratch_shapes=[pltpu.SemaphoreType.DMA((8,))],
        name="pack_parts",
    )(tokens, w_qkv, w_proj, w_merge)


def edges(tokens, above, below):
    shapes = jax.ShapeDtypeStruct((5, 72, 512), bf16), jax.ShapeDtypeStruct((32, 16, 512), bf16)
    return pl.pallas_call(
        edge_kernel,
        in_specs=[VMEM] * 3,
        out_specs=(VMEM, VMEM),
        out_shape=shapes,
        compiler_params=pltpu.CompilerParams(vmem_limit_bytes=32 << 20),
        cost_estimate=pl.CostEstimate(flops=212_000_000, bytes_accessed=3 << 20, transcendentals=0),
        name="edge_rows",
    )(tokens, above, below)


def attention_block(tokens, above, below, outer, gain, own_qkv, own_rest, sibling, merge_gain):
    perm = one_hot(centre_order(), 96)
    return pl.pallas_call(
        block_kernel,
        in_specs=[ANY, ANY, ANY, VMEM, VMEM, ANY, ANY, ANY] + [VMEM] * 5,
        out_specs=(ANY, VMEM),
        out_shape=(jax.ShapeDtypeStruct((2, 24, 24, 512), bf16), jax.ShapeDtypeStruct((288, 2048), bf16)),
        scratch_shapes=[
            pltpu.VMEM((2, 24, 24, 512), bf16),
            pltpu.VMEM((2, 30, 24, 512), bf16),
            pltpu.VMEM((16, 2, 16, 512), bf16),
            pltpu.VMEM((4, 16, 2, 16, 512), bf16),
            pltpu.SemaphoreType.DMA((17,)),
        ],
        compiler_params=pltpu.CompilerParams(vmem_limit_bytes=40 << 20),
        cost_estimate=pl.CostEstimate(flops=5_500_000_000, bytes_accessed=8 << 20, transcendentals=2_500_000),
        name="attention_block",
    )(tokens, above, below, outer, gain.reshape(1, 512), own_qkv, own_rest, sibling,
      jnp.asarray(perm), jnp.asarray(perm.T), jnp.asarray(edge_mask()), merge_gain.reshape(1, 2048),
      jnp.asarray(one_hot(merge_order(), 192)))


def merge_block(merged, own, pair, across, opposite, sibling, sibling_opposite):
    return pl.pallas_call(
        merge_kernel,
        in_specs=[VMEM] + [ANY] * 6,
        out_specs=VMEM,
        out_shape=jax.ShapeDtypeStruct((144, 2, 1024), bf16),
        scratch_shapes=[pltpu.VMEM((2, 16, 2, 4, 16, 512), bf16), pltpu.SemaphoreType.DMA((16,))],
        compiler_params=pltpu.CompilerParams(vmem_limit_bytes=24 << 20),
        cost_estimate=pl.CostEstimate(flops=1_200_000_000, bytes_accessed=8 << 20, transcendentals=0),
        name="merge_block",
    )(merged, own, pair, across, opposite, sibling, sibling_opposite)


def shift(block, axes, distance):
    devices = range(lax.axis_size(axes))
    route = [((i - distance) % len(devices), i) for i in devices]
    return lax.ppermute(block, axes, route)


def swap(block, axis, partner):
    return lax.ppermute(block, axis, list(enumerate(partner)))


def between_chips(block):
    devices = range(lax.axis_size(LON))
    return lax.ppermute(block, LON, [(i, (i + (1 if i % 2 else -1)) % len(devices)) for i in devices])


def together(*arrays):
    return lax.optimization_barrier(arrays)


def on_device(tokens, attn_gain, w_qkv, w_proj, merge_gain, w_merge):
    packed, top, bottom = pack(tokens, w_qkv, w_proj, w_merge)
    above = shift(bottom, LAT, 1)
    below = shift(top, LAT, -1)
    packed = lax.all_gather(packed, "zh")
    packed, above, below = together(packed, above, below)
    outer, inner = edges(tokens, above, below)
    outer = between_chips(outer)
    rest = lax.all_gather(packed[:, 3:], "y").reshape(16, 3, 16, 512)
    first, second = (1, 0, 3, 2), (3, 2, 1, 0)
    merge_own = rest[:, 1:]
    pair = swap(merge_own, "x", first)
    across = swap(merge_own, "x", second)
    qkv = lax.all_gather(packed[:, :3], "y").reshape(16, 3, 16, 512)
    pair, across, qkv = together(pair, across, qkv)
    across, outer = together(across, outer)
    opposite = swap(across, "x", first)
    sibling = shift(jnp.concatenate([qkv, rest[:, :1], inner.reshape(16, 2, 16, 512)], axis=1), "c", 1)
    sibling_merge = shift(jnp.stack([merge_own, pair, across]), "c", 1)
    fine, merged = attention_block(tokens, above, below, outer, attn_gain, qkv, rest, sibling, merge_gain)
    opposite, sibling_merge, merged = together(opposite, sibling_merge, merged)
    sibling_opposite = shift(opposite, "c", 1)
    coarse = merge_block(merged, rest, pair, across, opposite, sibling_merge, sibling_opposite)
    return fine, coarse.reshape(12, 12, 2, 1024).transpose(2, 0, 1, 3)


def solution(mesh):
    lat, lon = mesh.shape["lat"], mesh.shape["lon"]
    fine_mesh = Mesh(mesh.devices.reshape(lat // 4, 4, 4, lon // 8, 2), LAT + LON)
    in_specs = (P(None, LAT, LON, None), P(), P(LON, None), P(LON, None), P(), P(LON, None))
    out_specs = (P(None, LAT, LON, None), P(None, LAT, LON, None))
    return jax.shard_map(
        on_device, mesh=fine_mesh, in_specs=in_specs, out_specs=out_specs, check_vma=False
    )
```
